32 devices in a mesh: dp: 8 (over z, y), section: 4 (over x, core).
Axes of the slice: x: 2, y: 2, z: 4, core: 2. Of those that a mesh axis runs over, the one named last changes fastest.
Arguments:
- block_input: float32 [4, 8, 256, 512], P(None, 'dp'), may hold values from -20 to 20
- cotangent: float32 [4, 8, 256, 512], P(None, 'dp'), may hold values from -20 to 20
- section_weight: float32 [4, 512, 1024], P('section'), may hold values from -0.25 to 0.25
- section_vectors: float32 [8, 512], P('section'), may hold values from -6 to 1
- norm_params: float32 [4, 512], replicated, may hold values from 0.5 to 1.5
- running_stats: float32 [4, 512], replicated, may hold values from 0.5 to 2
- resets: int32 [4, 8, 4], P(None, 'dp'), may hold values from 1 to 255
- lengths: int32 [4, 8], P(None, 'dp'), may hold values from 128 to 256
Outputs:
- block_output: float32 [4, 8, 256, 512], P('section', 'dp')
- input_grad: float32 [4, 8, 256, 512], P('section', 'dp')
- section_weight_grad: float32 [4, 512, 1024], P('section')
- section_vectors_grad: float32 [8, 512], P('section')
- norm_grad: float32 [4, 512], P('section')
- new_running: float32 [4, 512], P('section')
The draws below stay inside these ranges and needn't reach their ends.
All inputs are finite; a program needn't handle non-finite values.
Results may differ from the reference program's by a relative error of at most 0.0003.
Values sent between devices are 32-bit elements; how exact they have to be, the bound alone decides.
A program may use at most 192 MiB of HBM per device.

```python
import jax
import jax.numpy as jnp
from jax import lax

D = 512
STATE = 256
LEN = 256
MICRO = 4
NRESET = 4
SECTIONS = 4
ROWS = 8


def row_scales(spread):
    positions = jnp.arange(ROWS, dtype=jnp.float32)
    return spread ** (positions / max(ROWS - 1, 1))


def draw_block_input(key, part):
    key = jax.random.fold_in(key, 11)
    noise_key = jax.random.fold_in(key, 0)
    full_shape = (MICRO, ROWS, LEN, D)
    return jnp.clip(jax.random.normal(noise_key, full_shape, jnp.float32), -4.0, 4.0) * row_scales(3.0)[None, :, None, None]


def draw_cotangent(key, part):
    key = jax.random.fold_in(key, 12)
    noise_key = jax.random.fold_in(key, 0)
    full_shape = (MICRO, ROWS, LEN, D)
    return jnp.clip(jax.random.normal(noise_key, full_shape, jnp.float32), -4.0, 4.0) * row_scales(3.0)[None, :, None, None]


def draw_section_vectors(key, part):
    key = jax.random.fold_in(key, 13)
    row_total = 2 * SECTIONS
    random_base = jax.random.uniform(key, (row_total, D), jnp.float32)
    row_kinds = jnp.arange(row_total)[:, None] % 4
    columns = jnp.arange(D)[None, :]
    skip_part = 2.0 * random_base - 1.0
    recurrent_part = jnp.where(columns < STATE, -6.0 + 6.5 * random_base, -3.0 + 3.5 * random_base)
    bias_part = random_base - 0.5
    return jnp.where(row_kinds == 0, skip_part, jnp.where(row_kinds == 1, recurrent_part, bias_part))


def with_ends(array, stream_key, low, largest):
    spot = [jax.random.randint(jax.random.fold_in(stream_key, axis), (), 0, length) for axis, length in enumerate(array.shape)]
    main_axis = array.shape.index(max(array.shape))
    beside = spot[:main_axis] + [(spot[main_axis] + 1) % array.shape[main_axis]] + spot[main_axis + 1:]
    return array.at[tuple(spot)].set(low).at[tuple(beside)].set(largest)


def block_levels(key, shape, cuts, smallest, top_value):
    loudness = 1.0
    for position, shards_of in cuts:
        draws = jax.random.uniform(jax.random.fold_in(jax.random.fold_in(key, 6), position), (shards_of,), jnp.float32, smallest / len(cuts), top_value / len(cuts))
        loudness = loudness * jnp.repeat(jnp.exp(draws), shape[position] // shards_of).reshape((-1,) + (1,) * (len(shape) - 1 - position))
    return loudness


def scatter_about(stream_key, extent, scale, reach, pieces=(), kind=jnp.bfloat16):
    gain = block_levels(stream_key, extent, pieces, -0.22, 0.18) if pieces else 1.0
    entries = jax.random.normal(stream_key, extent, jnp.float32) * scale * gain
    return jnp.minimum(jnp.maximum(entries, -reach), reach).astype(kind)


def setup_inputs(seed: int = 0) -> dict:
    key_list = jax.random.split(jax.random.key(seed), 9)
    return {
        "block_input": draw_block_input(jax.random.fold_in(key_list[8], 71), 0),
        "cotangent": draw_cotangent(jax.random.fold_in(key_list[8], 71), 0),
        "section_weight": scatter_about(key_list[2], (SECTIONS, D, 2 * D), D ** -0.5, 0.25, ((0, 4),), jnp.float32),
        "section_vectors": draw_section_vectors(jax.random.fold_in(key_list[8], 71), 0),
        "norm_params": jnp.clip(jax.random.uniform(key_list[4], (SECTIONS, D), jnp.float32, 0.5, 1.5), 0.5, 1.5),
        "running_stats": jnp.clip(jax.random.uniform(key_list[5], (SECTIONS, D), jnp.float32, 0.5, 2.0), 0.5, 2.0),
        "resets": with_ends(jax.random.randint(key_list[6], (MICRO, ROWS, NRESET), 1, LEN), jax.random.fold_in(key_list[6], 1), 1, LEN - 1).astype(jnp.int32),
        "lengths": with_ends(jax.random.randint(key_list[7], (MICRO, ROWS), LEN // 2, LEN + 1), jax.random.fold_in(key_list[7], 1), LEN // 2, LEN).astype(jnp.int32),
    }


epsilon = 1e-05
momentum = 0.1
highest = lax.Precision.HIGHEST

def row_masks(row_lengths, reset_marks, length):
    positions = jnp.arange(length, dtype=jnp.int32)
    usable = (positions[None, :] < row_lengths[:, None]).astype(jnp.float32)
    cleared = jnp.any(reset_marks[:, None, :] == positions[None, :, None], axis=-1).astype(jnp.float32)
    return (usable, cleared)

def project(values, weights):
    row_count, length, columns = values.shape
    flat = values.reshape(row_count * length, columns)
    return jnp.dot(flat, weights, precision=highest).reshape(row_count, length, weights.shape[1])

def recurrence(driven, cleared, rate_log, phase_log):
    state_count = rate_log.shape[0]
    radius = jnp.exp(-jnp.exp(rate_log))
    phases = jnp.exp(phase_log)
    scaling = jnp.sqrt(1.0 - radius * radius)
    turn_real = radius * jnp.cos(phases)
    turn_imag = radius * jnp.sin(phases)

    def advance(previous, inputs):
        state_real, state_imag = previous
        drive_now, clear_now = inputs
        keeping = (1.0 - clear_now)[:, None]
        new_real = keeping * (turn_real * state_real - turn_imag * state_imag) + scaling * drive_now[:, :state_count]
        new_imag = keeping * (turn_imag * state_real + turn_real * state_imag) + scaling * drive_now[:, state_count:]
        return ((new_real, new_imag), jnp.concatenate([new_real, new_imag], axis=-1))
    initial = jnp.zeros((driven.shape[0], state_count), driven.dtype)
    last_state, states = lax.scan(advance, (initial, initial), (jnp.swapaxes(driven, 0, 1), jnp.swapaxes(cleared, 0, 1)))
    return jnp.swapaxes(states, 0, 1)

def layer_forward(stream, usable, cleared, weights, vectors, norm_rows, layer_index):
    columns = stream.shape[-1]
    state_count = columns // 2
    weighting = usable[:, :, None]
    counted = jnp.sum(usable)
    center = lax.optimization_barrier(jnp.sum(weighting * stream, axis=(0, 1))) / counted
    spread = lax.optimization_barrier(jnp.sum(weighting * (stream - center) * (stream - center), axis=(0, 1))) / counted
    inverse = lax.rsqrt(spread + epsilon)
    normed = norm_rows[2 * layer_index] * (stream - center) * inverse + norm_rows[2 * layer_index + 1]
    mixer_weights = weights[2 * layer_index]
    driven = project(normed, mixer_weights[:, :columns])
    rates = vectors[4 * layer_index + 1]
    states = recurrence(driven, cleared, rates[:state_count], rates[state_count:])
    mixed = project(states, mixer_weights[:, columns:]) + vectors[4 * layer_index] * normed
    biases = jnp.concatenate([vectors[4 * layer_index + 2], vectors[4 * layer_index + 3]])
    joined = project(jax.nn.gelu(mixed, approximate=False), weights[2 * layer_index + 1]) + biases
    gated = joined[:, :, :columns] * jax.nn.sigmoid(joined[:, :, columns:])
    return (stream + weighting * gated, jnp.stack([center, spread]))

def reference(block_input, cotangent, section_weight, section_vectors, norm_params, running_stats, resets, lengths):
    micro_count, row_count, length, columns = block_input.shape
    layer_total = section_weight.shape[0] // 2

    def forward(block_in, weights, vectors, norm_rows):
        outputs = []
        layer_stats = []
        for micro_index in range(micro_count):
            usable, cleared = row_masks(lengths[micro_index], resets[micro_index], length)
            stream = block_in[micro_index]
            for layer_index in range(layer_total):
                stream, moments = layer_forward(stream, usable, cleared, weights, vectors, norm_rows, layer_index)
                layer_stats.append(moments)
            outputs.append(stream)
        return (jnp.stack(outputs), jnp.stack(layer_stats))
    block_output, pullback, layer_stats = jax.vjp(forward, block_input, section_weight, section_vectors, norm_params, has_aux=True)
    input_grad, weight_grad, vector_grad, norm_grad = pullback(cotangent)
    running = running_stats.reshape(layer_total, 2, columns)
    for micro_index in range(micro_count):
        running = (1.0 - momentum) * running + momentum * layer_stats[micro_index * layer_total:(micro_index + 1) * layer_total]
    return (block_output, input_grad, weight_grad, vector_grad, norm_grad, running.reshape(2 * layer_total, columns))
```

```python
import functools

import jax
import jax.numpy as jnp
from jax import lax
from jax.experimental import pallas as pl
from jax.experimental.pallas import tpu as pltpu
from jax.sharding import PartitionSpec as P

epsilon = 1e-05
momentum = 0.1
MESH = pl.DeviceIdType.MESH
f32 = jnp.float32
bf16 = jnp.bfloat16
ROWS = 16
UNIT = 256
BAND = 64
CHUNKS = 4
SEGMENTS = (
    ("glu1", 1.8), ("c1", 0.9), ("b1", 0.9), ("stream1", 1.5), ("gate0", 0.8), ("glu0", 1.8),
    ("mixed0", 2.0), ("states0", 0.6), ("c0", 0.9), ("scan0", 2.0), ("b0", 0.9), ("normed0", 1.5),
    ("stream0", 2.5),
)
MAKES = {
    "glu1": (1, 1, (0, 1, 2, 3)), "c1": (1, 0, (0, 1)), "b1": (1, 0, (2, 3)),
    "glu0": (0, 1, (0, 1, 2, 3)), "c0": (0, 0, (0, 1)), "b0": (0, 0, (2, 3)),
}


def far_first(layer, core, j):
    return layer != core


def turned(layer, core, j):
    return 0


def step_kinds(layer, core, j, k, owner):
    halving = [("halve", stage) for stage in range(k)]
    doubling = [("double", stage) for stage in reversed(range(k))]
    if far_first(layer, core, j):
        return [("core", 0)] + ([("far", 0)] + halving + doubling if owner else [])
    return [("core", 0)] + halving + ([("far", k)] + doubling if owner else [])


def planned(k):
    chunk, hop, work = 5.2, 1.5, 0.2
    roles = [(x, core) for x in range(2) for core in range(2)]
    links = {}
    ready = {role: {} for role in roles}
    order = {role: {name: [] for name, _ in SEGMENTS} | {"rest": []} for role in roles}
    now = dict.fromkeys(roles, 0.0)
    place = dict.fromkeys(roles, 0)
    early = {}

    def send(start, names, lasts):
        begin = max([start] + [links.get(name, 0.0) for name in names])
        for name in names:
            links[name] = begin + lasts
        return begin + lasts + hop

    def kinds(role, layer, j):
        return step_kinds(layer, role[1], j, k, role[0] == layer)

    def launch(role, layer, j, kind, stage, at):
        x, core = role
        if kind == "far":
            if x != layer:
                early[(1 - x, core), layer, j] = send(at, [("x", x)], chunk / (1 << stage))
            return
        bit = (stage + turned(layer, core, j)) % k
        lasts = chunk / (2 << stage)
        names = [(x, "z"), (x, "middle"), (x, "middle")] if bit == 2 and k == 3 else [(x, "z" if bit == 1 else bit)]
        for name in names[2:]:
            links[name] = links.get(name, 0.0) + lasts
        ready[role][layer, j] = (kinds(role, layer, j).index((kind, stage)), send(at, names[:2], lasts))

    def run(role, layer, j):
        step, at = ready[role].pop((layer, j))
        now[role] = max(now[role], at) + work
        place_in = SEGMENTS[place[role]][0] if place[role] < len(SEGMENTS) else "rest"
        order[role][place_in].append((layer, j, step))
        whole = step_kinds(layer, role[1], j, k, True)
        if step + 1 < len(whole):
            kind, stage = whole[step + 1]
            if kind == "far" and role[0] == layer:
                if (role, layer, j) in early:
                    ready[role][layer, j] = (step + 1, early[role, layer, j])
                else:
                    ready[role][layer, j] = (step + 1, None)
            elif kind == "far" or step + 1 < len(kinds(role, layer, j)):
                launch(role, layer, j, kind, stage, now[role])

    while True:
        for role in roles:
            for key, (step, at) in ready[role].items():
                if at is None and (role, *key) in early:
                    ready[role][key] = (step, early[(role, *key)])
        options = []
        for role in roles:
            working = place[role] < len(SEGMENTS)
            known = [
                (at + (3.0 if working and step > 0 else 0.0), key)
                for key, (step, at) in ready[role].items() if at is not None
            ]
            due = [(-key[0], at, key) for at, key in known if at <= now[role]]
            if due:
                options.append((now[role], role, min(due)[2]))
            elif working:
                options.append((now[role], role, None))
            elif known:
                options.append((min(known)[0], role, min(known)[1]))
        if not options:
            break
        _, role, key = min(options, key=lambda option: option[:2])
        if key is not None:
            run(role, *key)
            continue
        name, lasts = SEGMENTS[place[role]]
        place[role] += 1
        now[role] += lasts
        if name in MAKES and MAKES[name][1] != role[1]:
            layer, core, chunks = MAKES[name]
            for j in chunks:
                ready[role[0], core][layer, j] = (0, send(now[role], [("core", role)], chunk / 6))
    return order, now


def split(value):
    high = value.astype(bf16)
    return high, (value - high.astype(f32)).astype(bf16)


def fold(value):
    rows, columns = value.shape
    return jnp.sum(value.reshape(rows // 8, 8, columns), axis=0)


def kernel(n, T, D, *refs):
    (
        block_input, cotangent, matrix_in, vectors_in, norm_in, running_in, resets, lengths,
        out_ref, grad_ref, matrix_out, vector_out, norm_out, running_out,
        xs, g, W, wh, wl, nf, nh, nl, dr, sf, sh, sl, mx, dge, ah, al, jv, js, djh, djl,
        dmx, dmh, dml, dst, ddh, ddl, dn, G, SB, RB, R, V, tab, pw, masks, keep_lane, rowbuf,
        smsg, sbuf, tmp8, vmsg, vbuf, emsg, ebuf,
        XB, nth, ntl, sth, stl, ath, atl, af, coef, lams, gx, lsem, ws, wr, sibs, sibr, rss, rsr, ags, agr, sts, stq, secs, secr, vs, vr,
    ) = refs
    S = D // 2
    k = n.bit_length() - 1
    lanes = D // 128
    d = lax.axis_index("dp")
    s = lax.axis_index("section")
    x, c = s // 2, s % 2
    h = d % 2
    sibling = (d, 2 * x + (1 - c))
    far = (d, 2 * (1 - x) + c)
    pair = (d + 1 - 2 * h, s)

    def remote(src, dst, send, recv, device):
        return pltpu.make_async_remote_copy(
            src_ref=src, dst_ref=dst, send_sem=send, recv_sem=recv, device_id=device,
            device_id_type=MESH,
        )

    W2 = D // 2

    def rows_loop(body, init=None, step=ROWS, total=T, unroll=2):
        def wrapped(i, carry):
            result = body(pl.ds(pl.multiple_of(i * step, step), step), carry)
            return carry if result is None else result

        return lax.fori_loop(0, total // step, wrapped, 0 if init is None else init, unroll=unroll)

    load_x = pltpu.make_async_copy(block_input.at[s, 0], xs.at[0], lsem.at[0])
    load_g = pltpu.make_async_copy(cotangent.at[s, 0], g, lsem.at[1])
    load_w = [
        pltpu.make_async_copy(matrix_in.at[0, :, pl.ds(p * W2, W2)], W.at[s, p], lsem.at[2 + p])
        for p in range(CHUNKS)
    ]
    for copy in load_w:
        copy.start()
    load_x.start()
    load_g.start()

    barrier = pltpu.get_barrier_semaphore()

    def greet(j, carry):
        pl.semaphore_signal(
            barrier, inc=1, device_id=(lax.rem(d + j, n), s), device_id_type=MESH
        )
        return carry

    lax.fori_loop(1, n, greet, 0)
    for j in range(1, 4):
        pl.semaphore_signal(
            barrier, inc=1, device_id=(d, lax.rem(s + j, 4)), device_id_type=MESH
        )
    V[s] = vectors_in[...]

    length = lengths[0, s]
    marks = [resets[s, 0, i] for i in range(resets.shape[2])]
    token = lax.broadcasted_iota(jnp.int32, (T, 128), 0)
    place = token % 8

    def free(low, high):
        hit = None
        for mark in marks:
            inside = (mark >= low) & (mark <= high)
            hit = inside if hit is None else hit | inside
        return jnp.where(hit, 0.0, 1.0)

    for index, shift in enumerate((1, 2, 4)):
        masks[index] = jnp.where(place >= shift, free(token - shift + 1, token), 0.0)
        masks[4 + index] = jnp.where(place + shift <= 7, free(token + 1, token + shift), 0.0)
    masks[3] = free(token - place, token)
    masks[7] = free(token + 1, token - place + 8)
    keep_lane[...] = jnp.where(token > 0, free(token, token), 0.0)

    def usable_at(rows):
        spot = lax.broadcasted_iota(jnp.int32, (ROWS, 128), 0) + rows.start
        mask = jnp.where(spot < length, 1.0, 0.0).astype(f32)
        return jnp.concatenate([mask] * lanes, axis=1)

    def halves(mask):
        return jnp.concatenate([mask] * (S // 128), axis=1)

    count = jnp.full((1, D), length.astype(f32), f32)

    def send_round(index, tiles):
        def go(j, carry):
            remote(
                smsg.at[index, pl.ds(0, tiles)], sbuf.at[index, d, pl.ds(0, tiles)],
                sts.at[index, j], stq.at[index, j], (lax.rem(d + j, n), s),
            ).start()
            return carry

        lax.fori_loop(1, n, go, 0)

    def wait_round(index, tiles):
        def go(j, carry):
            remote(
                smsg.at[index, pl.ds(0, tiles)], sbuf.at[index, d, pl.ds(0, tiles)],
                sts.at[index, j], stq.at[index, j], (lax.rem(d + j, n), s),
            ).wait()
            return carry

        lax.fori_loop(1, n, go, 0)

    def pack(index, tile, first, second):
        for j in range(lanes):
            smsg[index, tile, j : j + 1, :] = first[:, 128 * j : 128 * j + 128]
            smsg[index, tile, lanes + j : lanes + j + 1, :] = second[:, 128 * j : 128 * j + 128]

    def unpack(value):
        tmp8[...] = value
        row = [tmp8[j : j + 1, :] for j in range(2 * lanes)]
        return jnp.concatenate(row[:lanes], axis=1), jnp.concatenate(row[lanes:], axis=1)

    def local_moments(layer):
        def first(rows, total):
            return total + fold(usable_at(rows) * xs[layer, rows, :])

        total = jnp.sum(rows_loop(first, jnp.zeros((8, D), f32)), axis=0, keepdims=True)
        mean = total / jnp.maximum(count, 1.0)

        def second(rows, squares):
            shifted = xs[layer, rows, :] - mean
            return squares + fold(usable_at(rows) * shifted * shifted)

        squares = jnp.sum(rows_loop(second, jnp.zeros((8, D), f32)), axis=0, keepdims=True)
        pack(layer, 0, total, squares)
        if layer == 0:
            smsg[0, 1] = jnp.full((8, 128), length.astype(f32), f32)

    def join_moments(layer):
        sbuf[layer, d, 0] = smsg[layer, 0]
        if layer == 0:
            sbuf[0, d, 1] = smsg[0, 1]

        def add(j, carry):
            return carry[0] + sbuf[layer, j, 0], carry[1] + sbuf[0, j, 1]

        zero = jnp.zeros((8, 128), f32)
        total, counted = lax.fori_loop(0, n, add, (zero, zero))
        tmp8[...] = total / counted
        center = tmp8[0:lanes, :]

        def between(j, carry):
            there = sbuf[0, j, 1][0:lanes, :]
            apart = sbuf[layer, j, 0][0:lanes, :] / jnp.maximum(there, 1.0) - center
            return carry + there * apart * apart

        apart = lax.fori_loop(0, n, between, jnp.zeros((lanes, 128), f32))
        center_row, spread_row = unpack(total / counted)
        tmp8[0:lanes, :] = apart / counted[0:lanes, :]
        apart_row = jnp.concatenate([tmp8[j : j + 1, :] for j in range(lanes)], axis=1)
        count_row = jnp.concatenate([counted[0:1, :]] * lanes, axis=1)
        return center_row, spread_row + apart_row, count_row

    quarter = D // 4

    def rows_of(q, p, half, core):
        start = pl.multiple_of((2 * half + core) * quarter, quarter)
        return W.at[q, p, pl.ds(start, quarter)]

    def own_copy(p):
        return remote(W.at[s, p], W.at[s, p], ws.at[0, p], wr.at[0, p], sibling)

    def far_copy_of(i):
        ref = rows_of(2 * x + i // CHUNKS, i % CHUNKS, h, c)
        return remote(ref, ref, ws.at[1, i], wr.at[1, i], far)

    def hand_copy(kind, i):
        half = 1 - h if kind == 4 else h
        ref = rows_of(2 * (1 - x) + i // CHUNKS, i % CHUNKS, half, c)
        return remote(ref, ref, ws.at[kind, i], wr.at[kind, i], pair if kind == 3 else sibling)

    def convert(q, p):
        def body(rows, carry):
            high, low = split(W[q, p, rows, :])
            wh[q, rows, p * W2 : p * W2 + W2] = high
            wl[q, rows, p * W2 : p * W2 + W2] = low

        rows_loop(body, total=D, unroll=4)

    def arrive(i):
        far_copy_of(i).wait_recv()
        hand_copy(2, i).start()
        hand_copy(3, i).start()

    def arrive_pair(i):
        hand_copy(3, i).wait_recv()
        hand_copy(4, i).start()

    def arrive_sibling(i):
        hand_copy(2, i).wait_recv()
        hand_copy(4, i).wait_recv()

    def send_far(i):
        far_copy_of(i).start()

    def convert_own():
        for q in range(2):
            for p in range(CHUNKS):
                convert(2 * x + q, p)

    def convert_far(plane, q, p):
        @pl.when(x == plane)
        def _():
            convert(q, p)

    events = []
    for i in range(2 * CHUNKS + 2):
        if i < 2 * CHUNKS:
            events.append((arrive, i))
        if 0 <= i - 1 < 2 * CHUNKS:
            events.append((arrive_pair, i - 1))
        if 0 <= i - 2 < 2 * CHUNKS:
            events.append((arrive_sibling, i - 2))
    passed = [0, 0]

    def until(plane, what):
        stop = events.index(what) + 1 if what is not None else len(events)
        todo = events[passed[plane] : stop]
        passed[plane] = max(passed[plane], stop)
        if todo:

            @pl.when(x == plane)
            def _():
                for event, i in todo:
                    event(i)

    def vector_copy(j):
        return remote(V.at[s], V.at[s], vs.at[j], vr.at[j], (d, lax.rem(s + j, 4)))

    def bit_value(task, stage):
        return 1 << ((stage + turned(*task)) % k)

    def my_bit(task, stage):
        return (d // bit_value(task, stage)) % 2

    def partner(task, stage):
        return (d + bit_value(task, stage) * (1 - 2 * my_bit(task, stage)), s)

    def segment(task, stage, mine):
        start = 0
        for earlier in range(stage):
            start = start + my_bit(task, earlier) * (D >> (earlier + 1))
        bit = my_bit(task, stage) if mine else 1 - my_bit(task, stage)
        size = D >> (stage + 1)
        return pl.ds(pl.multiple_of(start + bit * size, size), size)

    def landing(stage):
        size = D >> (stage + 1) if stage < k else D >> k
        return pl.ds(D - (D >> stage), size)

    def column(core, j):
        return j if core == 1 else (j + 2) % CHUNKS

    def sibling_copy(core, layer, j):
        return remote(
            G.at[2 * layer + 1 - core, column(1 - core, j)], SB.at[layer, j],
            sibs.at[layer, j], sibr.at[layer, j], sibling,
        )

    def mine_of(task):
        layer, core, j = task
        return G.at[2 * layer + core, column(core, j)]

    def halving_copy(task, stage):
        layer, core, j = task
        return remote(
            mine_of(task).at[segment(task, stage, False)], RB.at[layer, j, landing(stage)],
            rss.at[layer, j, stage], rsr.at[layer, j, stage], partner(task, stage),
        )

    def far_copy(task):
        layer, core, j = task
        if far_first(*task):
            source, target = mine_of(task), XB.at[j]
        else:
            source, target = mine_of(task).at[segment(task, k - 1, True)], RB.at[layer, j, landing(k)]
        return remote(source, target, rss.at[layer, j, k], rsr.at[layer, j, k], far)

    def doubling_copy(task, stage):
        layer, core, j = task
        ref = R.at[column(core, j), segment(task, stage, True)]
        return remote(ref, ref, ags.at[j, stage], agr.at[j, stage], partner(task, stage))

    def result_copy(j):
        return pltpu.make_async_copy(R.at[j], matrix_out.at[0, :, pl.ds(j * W2, W2)], lsem.at[6 + j])

    def add_rows(target, start, mine, mine_start, source, source_start, size):
        step = min(size, 32)

        def body(i, carry):
            a, b, e = (
                pl.ds(pl.multiple_of(first + i * step, 8), step)
                for first in (start, mine_start, source_start)
            )
            target[a, :] = mine[b, :] + source[e, :]
            return carry

        lax.fori_loop(0, size // step, body, 0, unroll=min(2, size // step))

    def advance(role, layer, j, step):
        plane, core = role
        task = (layer, core, j)
        whole = step_kinds(layer, core, j, k, True)
        kind, stage = whole[step]
        after = whole[step + 1] if step + 1 < len(whole) else None
        mine, total = mine_of(task), R.at[column(core, j)]
        target = total if after is not None and after[0] == "double" else mine
        if kind == "core":
            sibling_copy(core, layer, j).wait_recv()
            add_rows(target, 0, mine, 0, SB.at[layer, j], 0, D)
        elif kind == "far":
            far_copy(task).wait_recv()
            if far_first(*task):
                add_rows(target, 0, mine, 0, XB.at[j], 0, D)
            else:
                kept = segment(task, k - 1, True)
                add_rows(target, kept.start, mine, kept.start, RB.at[layer, j], landing(k).start, kept.size)
        elif kind == "halve":
            halving_copy(task, stage).wait()
            kept = segment(task, stage, True)
            add_rows(target, kept.start, mine, kept.start, RB.at[layer, j], landing(stage).start, kept.size)
        else:
            doubling_copy(task, stage).wait()
        if after is None:
            result_copy(column(core, j)).start()
        elif after[0] == "far":
            if plane != layer:
                far_copy(task).start()
        elif after[0] == "halve":
            halving_copy(task, after[1]).start()
        else:
            doubling_copy(task, after[1]).start()

    plans = planned(k)[0]

    def by_role(work):
        for role in plans:
            todo = work(role)
            if todo:

                @pl.when(s == 2 * role[0] + role[1])
                def _():
                    for layer, j, step in todo:
                        advance(role, layer, j, step)

    def steps_before(name):
        by_role(lambda role: plans[role][name])

    load_x.wait()
    local_moments(0)
    pl.semaphore_wait(barrier, n - 1 + 3)
    send_round(0, 2)
    for j in range(1, 4):
        vector_copy(j).start()
    for p in range(CHUNKS):
        load_w[p].wait()

        @pl.when(c == 0)
        def _():
            send_far(p)

        own_copy(p).start()
    for p in range(CHUNKS):
        own_copy(p).wait_recv()

        @pl.when(c == 1)
        def _():
            send_far(p)

    for p in range(CHUNKS):
        send_far(CHUNKS + p)
    for j in range(1, 4):
        vector_copy(j).wait()

    for layer in range(2):
        rates = V[2 * layer, 1:2, 0:S]
        angles = V[2 * layer, 1:2, S:D]
        grown = jnp.exp(rates)
        radius = jnp.exp(-grown)
        phases = jnp.exp(angles)
        cosine, sine = jnp.cos(phases), jnp.sin(phases)
        scaling = jnp.sqrt(1.0 - radius * radius)
        for index, row in enumerate((grown, radius, phases, cosine, sine, scaling)):
            coef[layer, index : index + 1, :] = row
        power = [(radius * cosine, radius * sine)]
        for _ in range(3):
            a, b = power[-1]
            power.append((a * a - b * b, 2.0 * a * b))
        for index, (a, b) in enumerate(power):
            pw[layer, 2 * index] = jnp.broadcast_to(a, (8, S))
            pw[layer, 2 * index + 1] = jnp.broadcast_to(b, (8, S))
        pw[layer, 8] = jnp.broadcast_to(scaling, (8, S))
        row = lax.broadcasted_iota(jnp.int32, (8, S), 0)
        for way, exponent in enumerate((row + 1, 8 - row)):
            a = jnp.ones((8, S), f32)
            b = jnp.zeros((8, S), f32)
            for index in range(4):
                on = (exponent // (1 << index)) % 2 == 1
                pa, pb = pw[layer, 2 * index], pw[layer, 2 * index + 1]
                a, b = jnp.where(on, a * pa - b * pb, a), jnp.where(on, a * pb + b * pa, b)
            tab[layer, 2 * way] = a
            tab[layer, 2 * way + 1] = b

    def forward_scan(layer):
        scale = pw[layer, 8]
        table_r, table_i = tab[layer, 0], tab[layer, 1]

        def body(i, carry):
            cr, ci = carry
            pieces = []
            for part in range(ROWS // 8):
                rows = pl.ds(pl.multiple_of(i * ROWS + part * 8, 8), 8)
                br = scale * dr[layer, rows, 0:S]
                bi = scale * dr[layer, rows, S:D]
                for index, shift in enumerate((1, 2, 4)):
                    mask = halves(masks[index, rows, :])
                    pr, pi = pw[layer, 2 * index], pw[layer, 2 * index + 1]
                    rr = mask * pltpu.roll(br, shift, 0)
                    ri = mask * pltpu.roll(bi, shift, 0)
                    br, bi = br + (pr * rr - pi * ri), bi + (pr * ri + pi * rr)
                whole = halves(masks[3, rows, :])
                mr, mi = whole * table_r, whole * table_i
                hr = br + (mr * cr - mi * ci)
                hi = bi + (mr * ci + mi * cr)
                er, ei = (jnp.broadcast_to(v[7:8, :], (8, S)) for v in (mr, mi))
                lr, li = (jnp.broadcast_to(v[7:8, :], (8, S)) for v in (br, bi))
                cr, ci = lr + (er * cr - ei * ci), li + (er * ci + ei * cr)
                pieces.append(jnp.concatenate([hr, hi], axis=1))
            both = jnp.concatenate(pieces, axis=0)
            rows = pl.ds(pl.multiple_of(i * ROWS, ROWS), ROWS)
            sf[layer, rows, :] = both
            high, low = split(both)
            sh[rows, :] = high
            sl[rows, :] = low
            return cr, ci

        zero = jnp.zeros((8, S), f32)
        lax.fori_loop(0, T // ROWS, body, (zero, zero), unroll=2)

    def backward_scan(layer):
        scale = pw[layer, 8]
        table_r, table_i = tab[layer, 2], tab[layer, 3]
        top = lax.broadcasted_iota(jnp.int32, (8, S), 0) == 0

        def body(i, carry):
            cr, ci, lam_r, lam_i, gam = carry
            pieces = [None] * (ROWS // 8)
            for part in reversed(range(ROWS // 8)):
                start = T - ROWS - i * ROWS + part * 8
                rows = pl.ds(pl.multiple_of(start, 8), 8)
                before = pl.ds(pl.multiple_of(jnp.maximum(start - 8, 0), 8), 8)
                br = dst[rows, 0:S]
                bi = dst[rows, S:D]
                for index, shift in enumerate((1, 2, 4)):
                    mask = halves(masks[4 + index, rows, :])
                    pr, pi = pw[layer, 2 * index], pw[layer, 2 * index + 1]
                    rr = mask * pltpu.roll(br, 8 - shift, 0)
                    ri = mask * pltpu.roll(bi, 8 - shift, 0)
                    br, bi = br + (pr * rr + pi * ri), bi + (pr * ri - pi * rr)
                whole = halves(masks[7, rows, :])
                mr, mi = whole * table_r, whole * table_i
                gr = br + (mr * cr + mi * ci)
                gi = bi + (mr * ci - mi * cr)
                er, ei = (jnp.broadcast_to(v[0:1, :], (8, S)) for v in (mr, mi))
                lr, li = (jnp.broadcast_to(v[0:1, :], (8, S)) for v in (br, bi))
                cr, ci = lr + (er * cr + ei * ci), li + (er * ci - ei * cr)
                keep = halves(keep_lane[rows, :])
                pr, pi = (
                    keep * jnp.where(
                        top, pltpu.roll(sf[layer, before, cut], 1, 0), pltpu.roll(sf[layer, rows, cut], 1, 0)
                    )
                    for cut in (slice(0, S), slice(S, D))
                )
                lam_r = lam_r + (gr * pr + gi * pi)
                lam_i = lam_i + (gi * pr - gr * pi)
                gam = gam + (gr * dr[layer, rows, 0:S] + gi * dr[layer, rows, S:D])
                pieces[part] = jnp.concatenate([scale * gr, scale * gi], axis=1)
            rows = pl.ds(pl.multiple_of(T - ROWS - i * ROWS, ROWS), ROWS)
            high, low = split(jnp.concatenate(pieces, axis=0))
            ddh[rows, :] = high
            ddl[rows, :] = low
            return cr, ci, lam_r, lam_i, gam

        zero = jnp.zeros((8, S), f32)
        _, _, lam_r, lam_i, gam = lax.fori_loop(
            0, T // ROWS, body, (zero,) * 5, unroll=2
        )
        for index, value in enumerate((lam_r, lam_i, gam)):
            lams[layer, index] = value

    def decay_back(layer):
        lam_r, lam_i, gam = (jnp.sum(lams[layer, index], axis=0, keepdims=True) for index in range(3))
        grown, radius, phases, cosine, sine, scaling = (
            coef[layer, index : index + 1, :] for index in range(6)
        )
        along = lam_r * cosine + lam_i * sine
        across = lam_i * cosine - lam_r * sine
        da = along - gam * radius / scaling
        vmsg[4 * layer + 1 : 4 * layer + 2, 0:S] = -radius * grown * da
        vmsg[4 * layer + 1 : 4 * layer + 2, S:D] = radius * phases * across

    tiles = [slice(i, i + D // 2) for i in range(0, D, D // 2)]

    def tile(index, start=0):
        return slice(start + index * UNIT, start + (index + 1) * UNIT)

    def multiply(left, right, depth, columns, keep, transpose=False):
        left_high, left_low = left
        parts = left_high.shape[0] // BAND
        pairs = columns // 2

        def run(*sums):
            def sum_of(pair, unit, part):
                return sums[((pair % 2) * 2 + unit) * parts + part]

            def pop(pair):
                for part in range(parts):
                    for unit in range(2):
                        keep(
                            2 * pair + unit, slice(part * BAND, part * BAND + BAND),
                            pltpu.matmul_pop(sum_of(pair, unit, part)),
                        )

            sequence = [
                (pair, step, low)
                for pair in range(pairs) for step in range(depth // UNIT) for low in range(2)
            ]

            def push(index):
                pair, step, low = sequence[index]
                for unit in range(2):
                    pltpu.matmul_push_rhs(
                        right(low, step, 2 * pair + unit), index % 2, unit, transpose=transpose
                    )

            push(0)
            for index, (pair, step, low) in enumerate(sequence):
                for turn, source in enumerate((left_high,) if low else (left_high, left_low)):
                    for part in range(parts):
                        first = turn == 0 and part == 0
                        rows = source[part * BAND : part * BAND + BAND, tile(step)]
                        for unit in range(2):
                            pltpu.matmul_acc_lhs(
                                sum_of(pair, unit, part), rows,
                                load_staged_rhs=index % 2 if first else None,
                            )
                        if first and index + 1 < len(sequence):
                            push(index + 1)
                if pair > 0 and step == 0 and low == 0:
                    pop(pair - 1)
            pop(pairs - 1)

        pl.run_scoped(
            run,
            *[pltpu.ACC(unit)((BAND, UNIT), f32) for _ in range(2) for unit in range(2) for _ in range(parts)],
        )

    def weight_tiles(q, start=0):
        return lambda part, step, column: (wh, wl)[part][q, tile(step), tile(column, start)]

    def weight_tiles_across(q, start=0):
        return lambda part, step, column: (wh, wl)[part][q, tile(column), tile(step, start)]

    def keep_in(ref):
        def keep(column, rows, value):
            ref[rows, tile(column)] = value

        return keep

    def forward(layer, center, inverse):
        gain = norm_in[2 * layer : 2 * layer + 1, :]
        offset = norm_in[2 * layer + 1 : 2 * layer + 2, :]
        skip = V[2 * layer, 0:1, :]
        mixer, glu = 2 * layer, 2 * layer + 1
        away = 1 - layer

        def normalise(rows, carry):
            normed = gain * ((xs[layer, rows, :] - center) * inverse) + offset
            nf[layer, rows, :] = normed
            high, low = split(normed)
            nh[rows, :] = high
            nl[rows, :] = low

        rows_loop(normalise)
        until(away, (arrive_sibling, 1))
        for p in range(2):
            convert_far(away, mixer, p)
        multiply((nh, nl), weight_tiles(mixer), D, D // UNIT, keep_in(dr.at[layer]))
        if layer == 0:
            until(0, (arrive, 1))
        forward_scan(layer)
        until(away, (arrive_sibling, 3))
        for p in range(2, 4):
            convert_far(away, mixer, p)
        multiply((sh, sl), weight_tiles(mixer, D), D, D // UNIT, keep_in(mx))
        until(away, (arrive, 5))
        if layer == 0:
            until(0, (arrive_pair, 1))

        def activate(rows, carry):
            mixed = mx[rows, :] + skip * nf[layer, rows, :]
            phi = 0.5 * (1.0 + lax.erf(mixed * 0.7071067811865476))
            dge[layer, rows, :] = phi + mixed * (0.3989422804014327 * jnp.exp(-0.5 * mixed * mixed))
            active = mixed * phi
            af[rows, :] = active
            high, low = split(active)
            ah[rows, :] = high
            al[rows, :] = low

        rows_loop(activate)
        for p in range(CHUNKS):
            until(away, (arrive_sibling, CHUNKS + p))
            convert_far(away, glu, p)
        multiply((ah, al), weight_tiles(glu), D, D // UNIT, keep_in(jv.at[layer]))
        multiply((ah, al), weight_tiles(glu, D), D, D // UNIT, keep_in(js.at[layer]))
        if layer == 0:
            until(0, (arrive_pair, 2))
        value_bias = V[2 * layer + 1, 0:1, :]
        gate_bias = V[2 * layer + 1, 1:2, :]
        target = xs.at[layer + 1]

        def gate(rows, carry):
            value = jv[layer, rows, :] + value_bias
            sig = 1.0 / (1.0 + jnp.exp(-(js[layer, rows, :] + gate_bias)))
            jv[layer, rows, :] = value
            js[layer, rows, :] = sig
            target[rows, :] = xs[layer, rows, :] + usable_at(rows) * (value * sig)

        rows_loop(gate)

    def gate_back(layer):
        def body(rows, carry):
            dgated = usable_at(rows) * g[rows, :]
            value, sig = jv[layer, rows, :], js[layer, rows, :]
            dvalue = dgated * sig
            dgate = dvalue * value * (1.0 - sig)
            for cut, part in ((slice(0, D), dvalue), (slice(D, 2 * D), dgate)):
                high, low = split(part)
                djh[rows, cut] = high
                djl[rows, cut] = low
            return carry[0] + fold(dvalue), carry[1] + fold(dgate)

        zero = jnp.zeros((8, D), f32)
        first, second = rows_loop(body, (zero, zero))
        vmsg[4 * layer + 2 : 4 * layer + 3, :] = jnp.sum(first, axis=0, keepdims=True)
        vmsg[4 * layer + 3 : 4 * layer + 4, :] = jnp.sum(second, axis=0, keepdims=True)

    def mixed_back(layer):
        glu = 2 * layer + 1
        multiply((djh, djl), weight_tiles_across(glu), 2 * D, D // UNIT, keep_in(dmx), transpose=True)

        def body(rows, skip_sum):
            dmixed = dge[layer, rows, :] * dmx[rows, :]
            dmx[rows, :] = dmixed
            high, low = split(dmixed)
            dmh[rows, :] = high
            dml[rows, :] = low
            return skip_sum + fold(dmixed * nf[layer, rows, :])

        skip_sum = rows_loop(body, jnp.zeros((8, D), f32))
        vmsg[4 * layer : 4 * layer + 1, :] = jnp.sum(skip_sum, axis=0, keepdims=True)

    def states_back(layer):
        multiply(
            (dmh, dml), weight_tiles_across(2 * layer, D), D, D // UNIT, keep_in(dst), transpose=True
        )

    def turn(layer):
        for source, high_ref, low_ref in ((nf.at[layer], nth, ntl), (sf.at[layer], sth, stl), (af, ath, atl)):
            for t in tiles:
                for u in range(0, T, 128):
                    high, low = split(source[u : u + 128, t].T)
                    high_ref[layer, t, u : u + 128] = high
                    low_ref[layer, t, u : u + 128] = low

    def weight_back(q, chunks, left, right, columns):
        def keep(column, rows, value):
            G[q, chunks[column], rows, :] = value

        multiply(
            left, lambda part, step, column: right[part][tile(step), tile(column)], T, columns, keep
        )

    def hand_over(core, layer, chunks):
        @pl.when(c == core)
        def _():
            for j in chunks:
                sibling_copy(core, layer, j).start()

    def glu_back(layer):
        weight_back(
            2 * layer + 1, range(CHUNKS), (ath.at[layer], atl.at[layer]), (djh, djl), CHUNKS
        )
        hand_over(0, layer, range(CHUNKS))

    def c_back(layer):
        weight_back(2 * layer, (2, 3), (sth.at[layer], stl.at[layer]), (dmh, dml), 2)
        hand_over(1, layer, (0, 1))

    def b_back(layer):
        weight_back(2 * layer, (0, 1), (nth.at[layer], ntl.at[layer]), (ddh, ddl), 2)
        hand_over(1, layer, (2, 3))

    def normed_back(layer, center, inverse):
        skip = V[2 * layer, 0:1, :]
        multiply((ddh, ddl), weight_tiles_across(2 * layer), D, D // UNIT, keep_in(dn), transpose=True)

        def body(rows, carry):
            dnormed = skip * dmx[rows, :] + dn[rows, :]
            dn[rows, :] = dnormed
            scaled = (xs[layer, rows, :] - center) * inverse
            return carry[0] + fold(dnormed * scaled), carry[1] + fold(dnormed)

        zero = jnp.zeros((8, D), f32)
        gain_sum, offset_sum = rows_loop(body, (zero, zero))
        pack(
            2 + layer, 0, jnp.sum(gain_sum, axis=0, keepdims=True),
            jnp.sum(offset_sum, axis=0, keepdims=True),
        )
        send_round(2 + layer, 1)

    def stream_back(layer, center, inverse, counted):
        wait_round(2 + layer, 1)
        sbuf[2 + layer, d, 0] = smsg[2 + layer, 0]
        total = lax.fori_loop(
            0, n, lambda j, carry: carry + sbuf[2 + layer, j, 0], jnp.zeros((8, 128), f32)
        )
        gain_total, offset_total = unpack(total)
        emsg[2 * layer, 2:3, :] = gain_total
        emsg[2 * layer + 1, 2:3, :] = offset_total
        factor = norm_in[2 * layer : 2 * layer + 1, :] * inverse
        gain_part, offset_part = gain_total / counted, offset_total / counted
        target = gx if layer == 0 else g

        def body(rows, carry):
            scaled = (xs[layer, rows, :] - center) * inverse
            usable = usable_at(rows)
            target[rows, :] = g[rows, :] + factor * (
                dn[rows, :] - usable * (offset_part + scaled * gain_part)
            )

        rows_loop(body)

    convert_own()
    wait_round(0, 2)
    for layer in range(2):
        if layer == 1:
            local_moments(1)
            send_round(1, 1)
            turn(0)
            until(0, (arrive_sibling, 1))
            wait_round(1, 1)
        center, spread, counted = join_moments(layer)
        emsg[2 * layer, 3:4, :] = center
        emsg[2 * layer + 1, 3:4, :] = spread
        inverse = lax.rsqrt(spread + epsilon)
        rowbuf[2 * layer : 2 * layer + 1, :] = center
        rowbuf[2 * layer + 1 : 2 * layer + 2, :] = inverse
        forward(layer, center, inverse)

    store_out = pltpu.make_async_copy(xs.at[2], out_ref, lsem.at[10])
    store_grad = pltpu.make_async_copy(gx, grad_ref, lsem.at[11])
    store_out.start()

    load_g.wait()
    center, inverse = rowbuf[2:3, :], rowbuf[3:4, :]
    gate_back(1)
    mixed_back(1)
    states_back(1)
    backward_scan(1)
    normed_back(1, center, inverse)
    turn(1)
    glu_back(1)
    steps_before("c1")
    c_back(1)
    steps_before("b1")
    b_back(1)
    steps_before("stream1")
    stream_back(1, center, inverse, counted)

    center, inverse = rowbuf[0:1, :], rowbuf[1:2, :]
    for name, work in (
        ("gate0", lambda: gate_back(0)),
        ("glu0", lambda: glu_back(0)),
        ("mixed0", lambda: mixed_back(0)),
        ("states0", lambda: states_back(0)),
        ("c0", lambda: c_back(0)),
        ("scan0", lambda: backward_scan(0)),
        ("b0", lambda: b_back(0)),
        ("normed0", lambda: normed_back(0, center, inverse)),
        ("stream0", lambda: stream_back(0, center, inverse, counted)),
    ):
        steps_before(name)
        work()

    store_grad.start()

    def vector_round(j):
        return remote(vmsg, vbuf.at[d], sts.at[4, j], stq.at[4, j], (lax.rem(d + j, n), s))

    for layer in range(2):
        decay_back(layer)

    def go(j, carry):
        vector_round(j).start()
        return carry

    def owner_copy(j):
        to = lax.rem(s + j, 4)
        return remote(emsg.at[to], ebuf.at[s], secs.at[j], secr.at[j], (d, to))

    lax.fori_loop(1, n, go, 0)
    def rest(part):
        def of(role):
            steps = plans[role]["rest"]
            cut = len(steps) // 3
            return steps[:cut] if part == 0 else steps[cut:]

        return of

    by_role(rest(0))

    def arrived(j, carry):
        vector_round(j).wait()
        return carry

    lax.fori_loop(1, n, arrived, 0)
    vbuf[d] = vmsg[...]
    total = lax.fori_loop(0, n, lambda j, carry: carry + vbuf[j], jnp.zeros((8, D), f32))
    for q in range(4):
        emsg[q, 0:2, :] = total[2 * q : 2 * q + 2, :]
    for j in range(1, 4):
        owner_copy(j).start()
    by_role(rest(1))

    for j in range(1, 4):
        owner_copy(j).wait()
    ebuf[s] = emsg[s]
    vector_total = jnp.zeros((2, D), f32)
    norm_total = jnp.zeros((1, D), f32)
    current = jnp.zeros((1, D), f32)
    for q in range(4):
        current = jnp.where(s == q, running_in[q : q + 1, :], current)
    for m in range(4):
        vector_total = vector_total + ebuf[m, 0:2, :]
        norm_total = norm_total + ebuf[m, 2:3, :]
        current = (1.0 - momentum) * current + momentum * ebuf[m, 3:4, :]
    vector_out[...] = vector_total
    norm_out[...] = norm_total
    running_out[...] = current

    for p in range(CHUNKS):
        own_copy(p).wait_send()
    for i in range(2 * CHUNKS):
        far_copy_of(i).wait_send()
        for kind in (2, 3, 4):
            hand_copy(kind, i).wait_send()
    for core in range(2):

        @pl.when(c == core)
        def _():
            for layer in range(2):
                for j in range(CHUNKS):
                    sibling_copy(core, layer, j).wait_send()

                    @pl.when(x != layer)
                    def _():
                        far_copy((layer, core, j)).wait_send()


    for j in range(CHUNKS):
        result_copy(j).wait()
    store_out.wait()
    store_grad.wait()


def finish(count, *refs):
    given, results, held, sems = refs[:count], refs[count : 2 * count], refs[2 * count : 3 * count], refs[-1]
    steps = [
        [pltpu.make_async_copy(a, b, sems.at[way, i]) for i, (a, b) in enumerate(zip(*pair))]
        for way, pair in enumerate(((given, held), (held, results)))
    ]
    for copy in steps[0]:
        copy.start()
    for first, second in zip(*steps):
        first.wait()
        second.start()
    for copy in steps[1]:
        copy.wait()


def solution(mesh):
    n = mesh.shape["dp"]
    k = n.bit_length() - 1
    assert mesh.shape["section"] == 4 and n == 1 << k and k >= 1

    def shards(block_input, cotangent, matrix, vectors, norm_params, running, resets, lengths):
        micro, rows, T, D = block_input.shape
        assert micro == 4 and rows == 1
        S = D // 2
        vmem = lambda shape, dtype=f32: pltpu.VMEM(shape, dtype)
        dma = lambda *shape: pltpu.SemaphoreType.DMA(shape)
        scratch = [
            vmem((3, T, D)), vmem((T, D)),
            vmem((4, 4, D, S)), vmem((4, D, 2 * D), bf16), vmem((4, D, 2 * D), bf16),
            vmem((2, T, D)), vmem((T, D), bf16), vmem((T, D), bf16),
            vmem((2, T, D)),
            vmem((2, T, D)), vmem((T, D), bf16), vmem((T, D), bf16),
            vmem((T, D)),
            vmem((2, T, D)),
            vmem((T, D), bf16), vmem((T, D), bf16),
            vmem((2, T, D)), vmem((2, T, D)),
            vmem((T, 2 * D), bf16), vmem((T, 2 * D), bf16),
            vmem((T, D)), vmem((T, D), bf16), vmem((T, D), bf16),
            vmem((T, D)),
            vmem((T, D), bf16), vmem((T, D), bf16),
            vmem((T, D)),
            vmem((4, 4, D, S)), vmem((2, 4, D, S)), vmem((2, 4, D, S)), vmem((4, D, S)),
            vmem((4, 2, D)),
            vmem((2, 4, 8, S)), vmem((2, 9, 8, S)),
            vmem((8, T, 128)), vmem((T, 128)),
            vmem((8, D)),
            vmem((4, 2, 8, 128)), vmem((4, n, 2, 8, 128)), vmem((8, 128)),
            vmem((8, D)), vmem((n, 8, D)), vmem((4, 4, D)), vmem((4, 4, D)),
            vmem((4, D, S)),
            *[vmem((2, D, T), bf16)] * 6,
            vmem((T, D)),
            vmem((2, 8, S)), vmem((2, 3, 8, S)),
            vmem((T, D)),
            dma(12), dma(5, 8), dma(5, 8), dma(2, 4), dma(2, 4),
            dma(2, 4, k + 1), dma(2, 4, k + 1), dma(4, k), dma(4, k),
            dma(5, n), dma(5, n), dma(4), dma(4), dma(4), dma(4),
        ]
        any_space = pl.BlockSpec(memory_space=pl.ANY)
        in_vmem = pl.BlockSpec(memory_space=pltpu.VMEM)
        in_smem = pl.BlockSpec(memory_space=pltpu.SMEM)
        shapes = (
            jax.ShapeDtypeStruct((T, D), f32),
            jax.ShapeDtypeStruct((T, D), f32),
            jax.ShapeDtypeStruct((1, D, 2 * D), f32),
            jax.ShapeDtypeStruct((2, D), f32),
            jax.ShapeDtypeStruct((1, D), f32),
            jax.ShapeDtypeStruct((1, D), f32),
        )
        results = pl.pallas_call(
            functools.partial(kernel, n, T, D),
            out_shape=shapes,
            in_specs=[any_space, any_space, any_space, in_vmem, in_vmem, in_vmem, in_smem, in_smem],
            out_specs=(any_space, any_space, any_space, in_vmem, in_vmem, in_vmem),
            scratch_shapes=scratch,
            compiler_params=pltpu.CompilerParams(
                collective_id=0, has_side_effects=True, vmem_limit_bytes=60 * 1024 * 1024
            ),
        )(block_input, cotangent, matrix, vectors, norm_params, running, resets, lengths.reshape(1, 4))
        out, grad, *rest = pl.pallas_call(
            functools.partial(finish, len(shapes)),
            out_shape=shapes,
            in_specs=[any_space] * len(shapes),
            out_specs=(any_space,) * len(shapes),
            scratch_shapes=[vmem(shape.shape) for shape in shapes] + [dma(2, len(shapes))],
        )(*results)
        return (out[None, None], grad[None, None], *rest)

    return jax.shard_map(
        shards,
        mesh=mesh,
        in_specs=(
            P(None, "dp", None, None),
            P(None, "dp", None, None),
            P("section", None, None),
            P("section", None),
            P(),
            P(),
            P(None, "dp", None),
            P(None, "dp"),
        ),
        out_specs=(
            P("section", "dp", None, None),
            P("section", "dp", None, None),
            P("section", None, None),
            P("section", None),
            P("section", None),
            P("section", None),
        ),
        check_vma=False,
    )
```

```python
import functools

import jax
import jax.numpy as jnp
from jax import lax
from jax.experimental import pallas as pl
from jax.experimental.pallas import tpu as pltpu
from jax.sharding import PartitionSpec as P

epsilon = 1e-05
momentum = 0.1
MESH = pl.DeviceIdType.MESH
f32 = jnp.float32
bf16 = jnp.bfloat16
ROWS = 16
UNIT = 256
BAND = 64
CHUNKS = 4
SEGMENTS = (
    ("glu1", 1.8), ("c1", 0.9), ("b1", 0.9), ("stream1", 1.5), ("gate0", 0.8), ("glu0", 1.8),
    ("mixed0", 2.0), ("states0", 0.6), ("c0", 0.9), ("scan0", 2.0), ("b0", 0.9), ("normed0", 1.5),
)
MAKES = {
    "glu1": (1, 1, (0, 1, 2, 3)), "c1": (1, 0, (0, 1)), "b1": (1, 0, (2, 3)),
    "glu0": (0, 1, (0, 1, 2, 3)), "c0": (0, 0, (0, 1)), "b0": (0, 0, (2, 3)),
}


METHODS = {(0, 0): "dddd", (0, 1): "xxxx", (1, 0): "xxxx", (1, 1): "dddd"}


def far_first(layer, core, j):
    return METHODS[layer, core][j] == "x"


def stages(k):
    found, bit = [(0, 2)], 1
    while bit < k:
        bits = min(2, k - bit)
        found.append((bit, 1 << bits))
        bit += bits
    return found


def step_kinds(layer, core, j, k, owner):
    count = len(stages(k))
    halving = [("halve", stage) for stage in range(count)]
    doubling = [("double", stage) for stage in reversed(range(count))]
    if far_first(layer, core, j):
        return [("core", 0)] + ([("far", 0)] + halving + doubling if owner else [])
    return [("core", 0)] + halving + ([("far", k)] + doubling if owner else [])


def planned(k):
    chunk, far_chunk, core_chunk, hop, work, slow = 4.9, 5.0, 0.85, 1.0, 0.2, 1.0
    roles = [(x, core) for x in range(2) for core in range(2)]
    links = {}
    ready = {role: {} for role in roles}
    order = {role: {name: [] for name, _ in SEGMENTS} | {"rest": []} for role in roles}
    now = dict.fromkeys(roles, 0.0)
    place = dict.fromkeys(roles, 0)
    early = {}

    def send(start, names, lasts):
        begin = max([start] + [links.get(name, 0.0) for name in names])
        for name in names:
            links[name] = begin + lasts
        return begin + lasts + hop

    def kinds(role, layer, j):
        return step_kinds(layer, role[1], j, k, role[0] == layer)

    def launch(role, layer, j, kind, stage, at):
        x, core = role
        if kind == "far":
            if x != layer:
                early[(1 - x, core), layer, j] = send(at, [("x", x)], far_chunk / (1 << stage))
            return
        share = 1.0
        for _, radix in stages(k)[:stage]:
            share /= radix
        radix = stages(k)[stage][1]
        end = send(at, [(x, stage)], chunk * share * (radix - 1) / radix)
        if radix == 4:
            end = max(end, send(at, [(x, stage, "middle")], chunk * share)) + 1.0
        ready[role][layer, j] = (kinds(role, layer, j).index((kind, stage)), end)

    def run(role, layer, j):
        step, at = ready[role].pop((layer, j))
        now[role] = max(now[role], at) + work
        place_in = SEGMENTS[place[role]][0] if place[role] < len(SEGMENTS) else "rest"
        order[role][place_in].append((layer, j, step))
        whole = step_kinds(layer, role[1], j, k, True)
        if step + 1 < len(whole):
            kind, stage = whole[step + 1]
            if kind == "far" and role[0] == layer:
                if (role, layer, j) in early:
                    ready[role][layer, j] = (step + 1, early[role, layer, j])
                else:
                    ready[role][layer, j] = (step + 1, None)
            elif kind == "far" or step + 1 < len(kinds(role, layer, j)):
                launch(role, layer, j, kind, stage, now[role])

    while True:
        for role in roles:
            for key, (step, at) in ready[role].items():
                if at is None and (role, *key) in early:
                    ready[role][key] = (step, early[(role, *key)])
        options = []
        for role in roles:
            working = place[role] < len(SEGMENTS)
            known = [
                (at + (1.0 if working and step > 0 else 0.0), key)
                for key, (step, at) in ready[role].items() if at is not None
            ]
            due = [(-key[0], at, key) for at, key in known if at <= now[role]]
            if due:
                options.append((now[role], role, min(due)[2]))
            elif working:
                options.append((now[role], role, None))
            elif known:
                options.append((min(known)[0], role, min(known)[1]))
        if not options:
            break
        _, role, key = min(options, key=lambda option: option[:2])
        if key is not None:
            run(role, *key)
            continue
        name, lasts = SEGMENTS[place[role]]
        place[role] += 1
        now[role] += lasts
        if name in MAKES and MAKES[name][1] != role[1]:
            layer, core, chunks = MAKES[name]
            for j in chunks:
                ready[role[0], core][layer, j] = (0, send(now[role], [("core", role)], core_chunk))
    return order, now


def split(value):
    high = value.astype(bf16)
    return high, (value - high.astype(f32)).astype(bf16)


def inverted(value):
    rough = pl.reciprocal(value, approx=True)
    rough = rough * (2.0 - value * rough)
    return rough * (2.0 - value * rough)


ERF_TOP = (
    -2.72614225801306e-10, 2.77068142495902e-08, -2.10102402082508e-06, -5.69250639462346e-05,
    -7.34990630326855e-04, -2.95459980854025e-03, -1.60960333262415e-02,
)
ERF_BOTTOM = (
    -1.45660718464996e-05, -2.13374055278905e-04, -1.68282697438203e-03, -7.37332916720468e-03,
    -1.42647390514189e-02,
)


def erf(value):
    value = jnp.clip(value, -3.832506856900711, 3.832506856900711)
    square = value * value
    top = bottom = None
    for factor in ERF_TOP:
        top = factor if top is None else top * square + factor
    for factor in ERF_BOTTOM:
        bottom = factor if bottom is None else bottom * square + factor
    return value * top * -inverted(-bottom)


def sigmoid(value):
    small = jnp.exp(-jnp.abs(value))
    share = inverted(1.0 + small)
    return jnp.where(value >= 0.0, share, small * share)


def fold(value):
    rows, columns = value.shape
    return jnp.sum(value.reshape(rows // 8, 8, columns), axis=0)


def kernel(n, T, D, *refs):
    (
        block_input, cotangent, matrix_in, vectors_in, norm_in, running_in, resets, lengths,
        out_ref, grad_ref, matrix_out, vector_out, norm_out, running_out,
        xs, g, W, wh, wl, nf, nh, nl, dr, sf, sh, sl, mx, dge, ah, al, jv, js, djh, djl,
        dmx, dmh, dml, dst, ddh, ddl, dn, G, SB, RB, R, V, tab, pw, masks, keep_lane, rowbuf,
        smsg, sbuf, tmp8, vmsg, vbuf, emsg, ebuf,
        XB, nth, ntl, sth, stl, ath, atl, af, coef, lams, gx, lsem, ws, wr, sibs, sibr, rss, rsr, ags, agr, sts, stq, secs, secr, vs, vr,
    ) = refs
    S = D // 2
    k = n.bit_length() - 1
    lanes = D // 128
    d = lax.axis_index("dp")
    s = lax.axis_index("section")
    x, c = s // 2, s % 2
    h = d % 2
    sibling = (d, 2 * x + (1 - c))
    far = (d, 2 * (1 - x) + c)
    pair = (d + 1 - 2 * h, s)

    def remote(src, dst, send, recv, device):
        return pltpu.make_async_remote_copy(
            src_ref=src, dst_ref=dst, send_sem=send, recv_sem=recv, device_id=device,
            device_id_type=MESH,
        )

    W2 = D // 2

    def rows_loop(body, init=None, step=ROWS, total=T, unroll=2):
        def wrapped(i, carry):
            result = body(pl.ds(pl.multiple_of(i * step, step), step), carry)
            return carry if result is None else result

        return lax.fori_loop(0, total // step, wrapped, 0 if init is None else init, unroll=unroll)

    load_x = pltpu.make_async_copy(block_input.at[s, 0], xs.at[0], lsem.at[0])
    load_g = pltpu.make_async_copy(cotangent.at[s, 0], g, lsem.at[1])
    load_w = [
        pltpu.make_async_copy(matrix_in.at[0, :, pl.ds(p * W2, W2)], W.at[s, p], lsem.at[2 + p])
        for p in range(CHUNKS)
    ]
    for copy in load_w:
        copy.start()
    load_x.start()
    load_g.start()

    barrier = pltpu.get_barrier_semaphore()

    def greet(j, carry):
        pl.semaphore_signal(
            barrier, inc=1, device_id=(lax.rem(d + j, n), s), device_id_type=MESH
        )
        return carry

    lax.fori_loop(1, n, greet, 0)
    for j in range(1, 4):
        pl.semaphore_signal(
            barrier, inc=1, device_id=(d, lax.rem(s + j, 4)), device_id_type=MESH
        )
    V[s] = vectors_in[...]

    length = lengths[0, s]
    marks = [resets[s, 0, i] for i in range(resets.shape[2])]
    token = lax.broadcasted_iota(jnp.int32, (T, 128), 0)
    place = token % 8

    def free(low, high):
        hit = None
        for mark in marks:
            inside = (mark >= low) & (mark <= high)
            hit = inside if hit is None else hit | inside
        return jnp.where(hit, 0.0, 1.0)

    for index, shift in enumerate((1, 2, 4)):
        masks[index] = jnp.where(place >= shift, free(token - shift + 1, token), 0.0)
        masks[4 + index] = jnp.where(place + shift <= 7, free(token + 1, token + shift), 0.0)
    masks[3] = free(token - place, token)
    masks[7] = free(token + 1, token - place + 8)
    keep_lane[...] = jnp.where(token > 0, free(token, token), 0.0)

    def usable_at(rows):
        spot = lax.broadcasted_iota(jnp.int32, (ROWS, 128), 0) + rows.start
        mask = jnp.where(spot < length, 1.0, 0.0).astype(f32)
        return jnp.concatenate([mask] * lanes, axis=1)

    def halves(mask):
        return jnp.concatenate([mask] * (S // 128), axis=1)

    count = jnp.full((1, D), length.astype(f32), f32)

    short = n <= 8

    def send_round(index, tiles):
        def go(j, carry):
            remote(
                smsg.at[index, pl.ds(0, tiles)], sbuf.at[index, d, pl.ds(0, tiles)],
                sts.at[index, j], stq.at[index, j], (lax.rem(d + j, n), s),
            ).start()
            return carry

        lax.fori_loop(1, n, go, 0, unroll=short)

    def wait_round(index, tiles, sent=False):
        def go(j, carry):
            copy = remote(
                smsg.at[index, pl.ds(0, tiles)], sbuf.at[index, d, pl.ds(0, tiles)],
                sts.at[index, j], stq.at[index, j], (lax.rem(d + j, n), s),
            )
            if sent:
                copy.wait_send()
            else:
                copy.wait_recv()
            return carry

        lax.fori_loop(1, n, go, 0, unroll=short)

    def pack(index, tile, first, second):
        for j in range(lanes):
            smsg[index, tile, j : j + 1, :] = first[:, 128 * j : 128 * j + 128]
            smsg[index, tile, lanes + j : lanes + j + 1, :] = second[:, 128 * j : 128 * j + 128]

    def unpack(value):
        tmp8[...] = value
        row = [tmp8[j : j + 1, :] for j in range(2 * lanes)]
        return jnp.concatenate(row[:lanes], axis=1), jnp.concatenate(row[lanes:], axis=1)

    def local_moments(layer, total=None):
        def first(rows, total):
            return total + fold(usable_at(rows) * xs[layer, rows, :])

        if total is None:
            total = rows_loop(first, jnp.zeros((8, D), f32))
        total = jnp.sum(total, axis=0, keepdims=True)
        mean = total / jnp.maximum(count, 1.0)

        def second(rows, squares):
            shifted = xs[layer, rows, :] - mean
            return squares + fold(usable_at(rows) * shifted * shifted)

        squares = jnp.sum(rows_loop(second, jnp.zeros((8, D), f32)), axis=0, keepdims=True)
        pack(layer, 0, total, squares)
        if layer == 0:
            smsg[0, 1] = jnp.full((8, 128), length.astype(f32), f32)

    def join_moments(layer):
        sbuf[layer, d, 0] = smsg[layer, 0]
        if layer == 0:
            sbuf[0, d, 1] = smsg[0, 1]

        def add(j, carry):
            return carry[0] + sbuf[layer, j, 0], carry[1] + sbuf[0, j, 1]

        zero = jnp.zeros((8, 128), f32)
        total, counted = lax.fori_loop(0, n, add, (zero, zero), unroll=short)
        tmp8[...] = total / counted
        center = tmp8[0:lanes, :]

        def between(j, carry):
            there = sbuf[0, j, 1][0:lanes, :]
            apart = sbuf[layer, j, 0][0:lanes, :] / jnp.maximum(there, 1.0) - center
            return carry + there * apart * apart

        apart = lax.fori_loop(0, n, between, jnp.zeros((lanes, 128), f32), unroll=short)
        center_row, spread_row = unpack(total / counted)
        tmp8[0:lanes, :] = apart / counted[0:lanes, :]
        apart_row = jnp.concatenate([tmp8[j : j + 1, :] for j in range(lanes)], axis=1)
        count_row = jnp.concatenate([counted[0:1, :]] * lanes, axis=1)
        return center_row, spread_row + apart_row, count_row

    quarter = D // 4

    def rows_of(q, p, half, core):
        start = pl.multiple_of((2 * half + core) * quarter, quarter)
        return W.at[q, p, pl.ds(start, quarter)]

    def own_copy(p):
        return remote(W.at[s, p], W.at[s, p], ws.at[0, p], wr.at[0, p], sibling)

    def far_copy_of(i):
        ref = rows_of(2 * x + i // CHUNKS, i % CHUNKS, h, c)
        return remote(ref, ref, ws.at[1, i], wr.at[1, i], far)

    def hand_copy(kind, i):
        half = 1 - h if kind == 4 else h
        ref = rows_of(2 * (1 - x) + i // CHUNKS, i % CHUNKS, half, c)
        return remote(ref, ref, ws.at[kind, i], wr.at[kind, i], pair if kind == 3 else sibling)

    def convert(q, p):
        def body(rows, carry):
            high, low = split(W[q, p, rows, :])
            wh[q, rows, p * W2 : p * W2 + W2] = high
            wl[q, rows, p * W2 : p * W2 + W2] = low

        rows_loop(body, total=D, unroll=4)

    def arrive(i):
        far_copy_of(i).wait_recv()
        hand_copy(2, i).start()
        hand_copy(3, i).start()

    def arrive_pair(i):
        hand_copy(3, i).wait_recv()
        hand_copy(4, i).start()

    def arrive_sibling(i):
        hand_copy(2, i).wait_recv()
        hand_copy(4, i).wait_recv()

    def send_far(i):
        far_copy_of(i).start()

    def convert_own():
        for q in range(2):
            for p in range(CHUNKS):
                convert(2 * x + q, p)

    def convert_far(plane, q, p):
        @pl.when(x == plane)
        def _():
            convert(q, p)

    events = ([], [])
    for i in range(2 * CHUNKS + 2):
        for plane in range(2):
            if i < 2 * CHUNKS:
                events[plane].append((arrive, i))
            if 0 <= i - 1 < 2 * CHUNKS:
                events[plane].append((arrive_pair, i - 1))
            if 0 <= i - 2 < 2 * CHUNKS:
                events[plane].append((arrive_sibling, i - 2))
    passed = [0, 0]

    def until(plane, what):
        stop = events[plane].index(what) + 1
        todo = events[plane][passed[plane] : stop]
        passed[plane] = max(passed[plane], stop)
        if todo:

            @pl.when(x == plane)
            def _():
                for event, i in todo:
                    event(i)

    def vector_copy(j):
        return remote(V.at[s], V.at[s], vs.at[j], vr.at[j], (d, lax.rem(s + j, 4)))

    levels = stages(k)
    sizes = [D]
    for _, radix in levels:
        sizes.append(sizes[-1] // radix)
    starts = [0]
    for (_, radix), size in zip(levels, sizes[1:]):
        starts.append(starts[-1] + (radix - 1) * size)

    def digit(stage):
        bit, radix = levels[stage]
        return (d // (1 << bit)) % radix

    def peer(stage, turn):
        bit, radix = levels[stage]
        place = (digit(stage) + turn) % radix
        return place, (d + (place - digit(stage)) * (1 << bit), s)

    def segment(stage, place=None):
        start = 0
        for earlier in range(stage):
            start = start + digit(earlier) * sizes[earlier + 1]
        start = start + (digit(stage) if place is None else place) * sizes[stage + 1]
        return pl.ds(pl.multiple_of(start, sizes[stage + 1]), sizes[stage + 1])

    def landing(stage, turn=1):
        if stage == len(levels):
            return pl.ds(starts[stage], sizes[stage])
        return pl.ds(starts[stage] + (turn - 1) * sizes[stage + 1], sizes[stage + 1])

    last = len(levels) - 1

    def column(core, j):
        return j if core == 1 else (j + 2) % CHUNKS

    def sibling_copy(core, layer, j):
        return remote(
            G.at[2 * layer + 1 - core, column(1 - core, j)], SB.at[layer, j],
            sibs.at[layer, j], sibr.at[layer, j], sibling,
        )

    def mine_of(task):
        layer, core, j = task
        return G.at[2 * layer + core, column(core, j)]

    def halving_copies(task, stage):
        layer, core, j = task
        copies = []
        for turn in range(1, levels[stage][1]):
            place, device = peer(stage, turn)
            copies.append(remote(
                mine_of(task).at[segment(stage, place)], RB.at[layer, j, landing(stage, turn)],
                rss.at[layer, j, 3 * stage + turn], rsr.at[layer, j, 3 * stage + turn], device,
            ))
        return copies

    def far_copy(task):
        layer, core, j = task
        if far_first(*task):
            source, target = mine_of(task), XB.at[j]
        else:
            source, target = mine_of(task).at[segment(last)], RB.at[layer, j, landing(last + 1)]
        return remote(source, target, rss.at[layer, j, 0], rsr.at[layer, j, 0], far)

    def doubling_copies(task, stage):
        layer, core, j = task
        ref = R.at[column(core, j), segment(stage)]
        return [
            remote(
                ref, ref, ags.at[j, 3 * stage + turn], agr.at[j, 3 * stage + turn], peer(stage, turn)[1]
            )
            for turn in range(1, levels[stage][1])
        ]

    def result_copy(j):
        return pltpu.make_async_copy(R.at[j], matrix_out.at[0, :, pl.ds(j * W2, W2)], lsem.at[6 + j])

    def add_rows(target, start, mine, sources, size):
        step = min(size, 32)

        def body(i, carry):
            rows = pl.ds(pl.multiple_of(start + i * step, 8), step)
            total = mine[rows, :]
            for source, first in sources:
                total = total + source[pl.ds(pl.multiple_of(first + i * step, 8), step), :]
            target[rows, :] = total
            return carry

        lax.fori_loop(0, size // step, body, 0, unroll=min(2, size // step))

    def advance(role, layer, j, step):
        plane, core = role
        task = (layer, core, j)
        whole = step_kinds(layer, core, j, k, True)
        kind, stage = whole[step]
        after = whole[step + 1] if step + 1 < len(whole) else None
        mine, total = mine_of(task), R.at[column(core, j)]
        target = total if after is not None and after[0] == "double" else mine
        if kind == "core":
            sibling_copy(core, layer, j).wait_recv()
            add_rows(target, 0, mine, [(SB.at[layer, j], 0)], D)
        elif kind == "far":
            far_copy(task).wait_recv()
            if far_first(*task):
                add_rows(target, 0, mine, [(XB.at[j], 0)], D)
            else:
                kept, source = segment(last), (RB.at[layer, j], landing(last + 1).start)
                add_rows(target, kept.start, mine, [source], kept.size)
        elif kind == "halve":
            for copy in halving_copies(task, stage):
                copy.wait()
            kept = segment(stage)
            sources = [
                (RB.at[layer, j], landing(stage, turn).start) for turn in range(1, levels[stage][1])
            ]
            add_rows(target, kept.start, mine, sources, kept.size)
        else:
            for copy in doubling_copies(task, stage):
                copy.wait()
        if after is None:
            result_copy(column(core, j)).start()
        elif after[0] == "far":
            if plane != layer:
                far_copy(task).start()
        else:
            copies = halving_copies if after[0] == "halve" else doubling_copies
            for copy in copies(task, after[1]):
                copy.start()

    plans = planned(k)[0]

    def by_role(work):
        for role in plans:
            todo = work(role)
            if todo:

                @pl.when(s == 2 * role[0] + role[1])
                def _():
                    for layer, j, step in todo:
                        advance(role, layer, j, step)

    def steps_before(name):
        by_role(lambda role: plans[role][name])

    load_x.wait()
    local_moments(0)
    pl.semaphore_wait(barrier, n - 1 + 3)
    send_round(0, 2)
    for j in range(1, 4):
        vector_copy(j).start()
    for p in range(CHUNKS):
        load_w[p].wait()

        @pl.when(c == 0)
        def _():
            send_far(p)

        own_copy(p).start()
    for p in range(CHUNKS):
        own_copy(p).wait_recv()

        @pl.when(c == 1)
        def _():
            send_far(p)

    for p in range(CHUNKS):
        send_far(CHUNKS + p)
    for j in range(1, 4):
        vector_copy(j).wait()

    for layer in range(2):
        rates = V[2 * layer, 1:2, 0:S]
        angles = V[2 * layer, 1:2, S:D]
        grown = jnp.exp(rates)
        radius = jnp.exp(-grown)
        phases = jnp.exp(angles)
        cosine, sine = jnp.cos(phases), jnp.sin(phases)
        scaling = jnp.sqrt(1.0 - radius * radius)
        for index, row in enumerate((grown, radius, phases, cosine, sine, scaling)):
            coef[layer, index : index + 1, :] = row
        power = [(radius * cosine, radius * sine)]
        for _ in range(3):
            a, b = power[-1]
            power.append((a * a - b * b, 2.0 * a * b))
        for index, (a, b) in enumerate(power):
            pw[layer, 2 * index] = jnp.broadcast_to(a, (8, S))
            pw[layer, 2 * index + 1] = jnp.broadcast_to(b, (8, S))
        pw[layer, 8] = jnp.broadcast_to(scaling, (8, S))
        row = lax.broadcasted_iota(jnp.int32, (8, S), 0)
        for way, exponent in enumerate((row + 1, 8 - row)):
            a = jnp.ones((8, S), f32)
            b = jnp.zeros((8, S), f32)
            for index in range(4):
                on = (exponent // (1 << index)) % 2 == 1
                pa, pb = pw[layer, 2 * index], pw[layer, 2 * index + 1]
                a, b = jnp.where(on, a * pa - b * pb, a), jnp.where(on, a * pb + b * pa, b)
            tab[layer, 2 * way] = a
            tab[layer, 2 * way + 1] = b

    def forward_scan(layer):
        scale = pw[layer, 8]
        table_r, table_i = tab[layer, 0], tab[layer, 1]

        def body(i, carry):
            cr, ci = carry
            pieces = []
            for part in range(ROWS // 8):
                rows = pl.ds(pl.multiple_of(i * ROWS + part * 8, 8), 8)
                br = scale * dr[layer, rows, 0:S]
                bi = scale * dr[layer, rows, S:D]
                for index, shift in enumerate((1, 2, 4)):
                    mask = halves(masks[index, rows, :])
                    pr, pi = pw[layer, 2 * index], pw[layer, 2 * index + 1]
                    rr = mask * pltpu.roll(br, shift, 0)
                    ri = mask * pltpu.roll(bi, shift, 0)
                    br, bi = br + (pr * rr - pi * ri), bi + (pr * ri + pi * rr)
                whole = halves(masks[3, rows, :])
                mr, mi = whole * table_r, whole * table_i
                hr = br + (mr * cr - mi * ci)
                hi = bi + (mr * ci + mi * cr)
                er, ei = (jnp.broadcast_to(v[7:8, :], (8, S)) for v in (mr, mi))
                lr, li = (jnp.broadcast_to(v[7:8, :], (8, S)) for v in (br, bi))
                cr, ci = lr + (er * cr - ei * ci), li + (er * ci + ei * cr)
                pieces.append(jnp.concatenate([hr, hi], axis=1))
            both = jnp.concatenate(pieces, axis=0)
            rows = pl.ds(pl.multiple_of(i * ROWS, ROWS), ROWS)
            sf[layer, rows, :] = both
            high, low = split(both)
            sh[rows, :] = high
            sl[rows, :] = low
            return cr, ci

        zero = jnp.zeros((8, S), f32)
        lax.fori_loop(0, T // ROWS, body, (zero, zero), unroll=2)

    def backward_scan(layer):
        scale = pw[layer, 8]
        table_r, table_i = tab[layer, 2], tab[layer, 3]
        top = lax.broadcasted_iota(jnp.int32, (8, S), 0) == 0

        def body(i, carry):
            cr, ci, lam_r, lam_i, gam = carry
            pieces = [None] * (ROWS // 8)
            for part in reversed(range(ROWS // 8)):
                start = T - ROWS - i * ROWS + part * 8
                rows = pl.ds(pl.multiple_of(start, 8), 8)
                before = pl.ds(pl.multiple_of(jnp.maximum(start - 8, 0), 8), 8)
                br = dst[rows, 0:S]
                bi = dst[rows, S:D]
                for index, shift in enumerate((1, 2, 4)):
                    mask = halves(masks[4 + index, rows, :])
                    pr, pi = pw[layer, 2 * index], pw[layer, 2 * index + 1]
                    rr = mask * pltpu.roll(br, 8 - shift, 0)
                    ri = mask * pltpu.roll(bi, 8 - shift, 0)
                    br, bi = br + (pr * rr + pi * ri), bi + (pr * ri - pi * rr)
                whole = halves(masks[7, rows, :])
                mr, mi = whole * table_r, whole * table_i
                gr = br + (mr * cr + mi * ci)
                gi = bi + (mr * ci - mi * cr)
                er, ei = (jnp.broadcast_to(v[0:1, :], (8, S)) for v in (mr, mi))
                lr, li = (jnp.broadcast_to(v[0:1, :], (8, S)) for v in (br, bi))
                cr, ci = lr + (er * cr + ei * ci), li + (er * ci - ei * cr)
                keep = halves(keep_lane[rows, :])
                pr, pi = (
                    keep * jnp.where(
                        top, pltpu.roll(sf[layer, before, cut], 1, 0), pltpu.roll(sf[layer, rows, cut], 1, 0)
                    )
                    for cut in (slice(0, S), slice(S, D))
                )
                lam_r = lam_r + (gr * pr + gi * pi)
                lam_i = lam_i + (gi * pr - gr * pi)
                gam = gam + (gr * dr[layer, rows, 0:S] + gi * dr[layer, rows, S:D])
                pieces[part] = jnp.concatenate([scale * gr, scale * gi], axis=1)
            rows = pl.ds(pl.multiple_of(T - ROWS - i * ROWS, ROWS), ROWS)
            high, low = split(jnp.concatenate(pieces, axis=0))
            ddh[rows, :] = high
            ddl[rows, :] = low
            return cr, ci, lam_r, lam_i, gam

        zero = jnp.zeros((8, S), f32)
        _, _, lam_r, lam_i, gam = lax.fori_loop(
            0, T // ROWS, body, (zero,) * 5, unroll=2
        )
        for index, value in enumerate((lam_r, lam_i, gam)):
            lams[layer, index] = value

    def decay_back(layer):
        lam_r, lam_i, gam = (jnp.sum(lams[layer, index], axis=0, keepdims=True) for index in range(3))
        grown, radius, phases, cosine, sine, scaling = (
            coef[layer, index : index + 1, :] for index in range(6)
        )
        along = lam_r * cosine + lam_i * sine
        across = lam_i * cosine - lam_r * sine
        da = along - gam * radius / scaling
        vmsg[4 * layer + 1 : 4 * layer + 2, 0:S] = -radius * grown * da
        vmsg[4 * layer + 1 : 4 * layer + 2, S:D] = radius * phases * across

    tiles = [slice(i, i + D // 2) for i in range(0, D, D // 2)]

    def tile(index, start=0):
        return slice(start + index * UNIT, start + (index + 1) * UNIT)

    def multiply(left, right, depth, columns, keep, transpose=False):
        left_high, left_low = left
        parts = left_high.shape[0] // BAND
        pairs = columns // 2

        def run(*sums):
            def sum_of(pair, unit, part):
                return sums[((pair % 2) * 2 + unit) * parts + part]

            def pop(pair):
                for part in range(parts):
                    for unit in range(2):
                        keep(
                            2 * pair + unit, slice(part * BAND, part * BAND + BAND),
                            pltpu.matmul_pop(sum_of(pair, unit, part)),
                        )

            sequence = [
                (pair, step, low)
                for pair in range(pairs) for step in range(depth // UNIT) for low in range(2)
            ]

            def push(index):
                pair, step, low = sequence[index]
                for unit in range(2):
                    pltpu.matmul_push_rhs(
                        right(low, step, 2 * pair + unit), index % 2, unit, transpose=transpose
                    )

            push(0)
            for index, (pair, step, low) in enumerate(sequence):
                for turn, source in enumerate((left_high,) if low else (left_high, left_low)):
                    for part in range(parts):
                        first = turn == 0 and part == 0
                        rows = source[part * BAND : part * BAND + BAND, tile(step)]
                        for unit in range(2):
                            pltpu.matmul_acc_lhs(
                                sum_of(pair, unit, part), rows,
                                load_staged_rhs=index % 2 if first else None,
                            )
                        if first and index + 1 < len(sequence):
                            push(index + 1)
                if pair > 0 and step == 0 and low == 0:
                    pop(pair - 1)
            pop(pairs - 1)

        pl.run_scoped(
            run,
            *[pltpu.ACC(unit)((BAND, UNIT), f32) for _ in range(2) for unit in range(2) for _ in range(parts)],
        )

    def weight_tiles(q, start=0):
        return lambda part, step, column: (wh, wl)[part][q, tile(step), tile(column, start)]

    def weight_tiles_across(q, start=0):
        return lambda part, step, column: (wh, wl)[part][q, tile(column), tile(step, start)]

    def keep_in(ref):
        def keep(column, rows, value):
            ref[rows, tile(column)] = value

        return keep

    def forward(layer, center, inverse):
        gain = norm_in[2 * layer : 2 * layer + 1, :]
        offset = norm_in[2 * layer + 1 : 2 * layer + 2, :]
        skip = V[2 * layer, 0:1, :]
        mixer, glu = 2 * layer, 2 * layer + 1
        away = 1 - layer

        def normalise(rows, carry):
            normed = gain * ((xs[layer, rows, :] - center) * inverse) + offset
            nf[layer, rows, :] = normed
            high, low = split(normed)
            nh[rows, :] = high
            nl[rows, :] = low

        rows_loop(normalise)
        until(away, (arrive_sibling, 1))
        for p in range(2):
            convert_far(away, mixer, p)
        multiply((nh, nl), weight_tiles(mixer), D, D // UNIT, keep_in(dr.at[layer]))
        if layer == 0:
            until(0, (arrive, 1))
        forward_scan(layer)
        until(away, (arrive_sibling, 3))
        for p in range(2, 4):
            convert_far(away, mixer, p)
        multiply((sh, sl), weight_tiles(mixer, D), D, D // UNIT, keep_in(mx))
        until(away, (arrive, 5))
        if layer == 0:
            until(0, (arrive_pair, 1))

        def activate(rows, carry):
            mixed = mx[rows, :] + skip * nf[layer, rows, :]
            phi = 0.5 * (1.0 + erf(mixed * 0.7071067811865476))
            dge[layer, rows, :] = phi + mixed * (0.3989422804014327 * jnp.exp(-0.5 * mixed * mixed))
            active = mixed * phi
            af[rows, :] = active
            high, low = split(active)
            ah[rows, :] = high
            al[rows, :] = low

        rows_loop(activate)
        for p in range(CHUNKS):
            until(away, (arrive_sibling, CHUNKS + p))
            convert_far(away, glu, p)
        multiply((ah, al), weight_tiles(glu), D, D // UNIT, keep_in(jv.at[layer]))
        multiply((ah, al), weight_tiles(glu, D), D, D // UNIT, keep_in(js.at[layer]))
        if layer == 0:
            until(0, (arrive_pair, 2))
        value_bias = V[2 * layer + 1, 0:1, :]
        gate_bias = V[2 * layer + 1, 1:2, :]
        target = xs.at[layer + 1]

        def gate(rows, carry):
            value = jv[layer, rows, :] + value_bias
            sig = sigmoid(js[layer, rows, :] + gate_bias)
            jv[layer, rows, :] = value
            js[layer, rows, :] = sig
            usable = usable_at(rows)
            result = xs[layer, rows, :] + usable * (value * sig)
            target[rows, :] = result
            return carry + fold(usable * result)

        return rows_loop(gate, jnp.zeros((8, D), f32))

    def gate_back(layer):
        def body(rows, carry):
            dgated = usable_at(rows) * g[rows, :]
            value, sig = jv[layer, rows, :], js[layer, rows, :]
            dvalue = dgated * sig
            dgate = dvalue * value * (1.0 - sig)
            for cut, part in ((slice(0, D), dvalue), (slice(D, 2 * D), dgate)):
                high, low = split(part)
                djh[rows, cut] = high
                djl[rows, cut] = low
            return carry[0] + fold(dvalue), carry[1] + fold(dgate)

        zero = jnp.zeros((8, D), f32)
        first, second = rows_loop(body, (zero, zero))
        vmsg[4 * layer + 2 : 4 * layer + 3, :] = jnp.sum(first, axis=0, keepdims=True)
        vmsg[4 * layer + 3 : 4 * layer + 4, :] = jnp.sum(second, axis=0, keepdims=True)

    def mixed_back(layer):
        glu = 2 * layer + 1
        multiply((djh, djl), weight_tiles_across(glu), 2 * D, D // UNIT, keep_in(dmx), transpose=True)

        def body(rows, skip_sum):
            dmixed = dge[layer, rows, :] * dmx[rows, :]
            dmx[rows, :] = dmixed
            high, low = split(dmixed)
            dmh[rows, :] = high
            dml[rows, :] = low
            return skip_sum + fold(dmixed * nf[layer, rows, :])

        skip_sum = rows_loop(body, jnp.zeros((8, D), f32))
        vmsg[4 * layer : 4 * layer + 1, :] = jnp.sum(skip_sum, axis=0, keepdims=True)

    def states_back(layer):
        multiply(
            (dmh, dml), weight_tiles_across(2 * layer, D), D, D // UNIT, keep_in(dst), transpose=True
        )

    def turn(layer):
        for source, high_ref, low_ref in ((nf.at[layer], nth, ntl), (sf.at[layer], sth, stl), (af, ath, atl)):
            for t in tiles:
                for u in range(0, T, 128):
                    high, low = split(source[u : u + 128, t].T)
                    high_ref[layer, t, u : u + 128] = high
                    low_ref[layer, t, u : u + 128] = low

    def weight_back(q, chunks, left, right, columns, first=0):
        def keep(column, rows, value):
            G[q, chunks[column], rows, :] = value

        multiply(
            left, lambda part, step, column: right[part][tile(step), tile(first + column)], T, columns, keep
        )

    def hand_over(core, layer, chunks):
        @pl.when(c == core)
        def _():
            for j in chunks:
                sibling_copy(core, layer, j).start()

    def glu_back(layer):
        for pair in range(2):
            chunks = (2 * pair, 2 * pair + 1)
            weight_back(
                2 * layer + 1, chunks, (ath.at[layer], atl.at[layer]), (djh, djl), 2, 2 * pair
            )
            hand_over(0, layer, chunks)

    def c_back(layer):
        weight_back(2 * layer, (2, 3), (sth.at[layer], stl.at[layer]), (dmh, dml), 2)
        hand_over(1, layer, (0, 1))

    def b_back(layer):
        weight_back(2 * layer, (0, 1), (nth.at[layer], ntl.at[layer]), (ddh, ddl), 2)
        hand_over(1, layer, (2, 3))

    def normed_back(layer, center, inverse):
        skip = V[2 * layer, 0:1, :]
        multiply((ddh, ddl), weight_tiles_across(2 * layer), D, D // UNIT, keep_in(dn), transpose=True)

        def body(rows, carry):
            dnormed = skip * dmx[rows, :] + dn[rows, :]
            dn[rows, :] = dnormed
            scaled = (xs[layer, rows, :] - center) * inverse
            return carry[0] + fold(dnormed * scaled), carry[1] + fold(dnormed)

        zero = jnp.zeros((8, D), f32)
        gain_sum, offset_sum = rows_loop(body, (zero, zero))
        pack(
            2 + layer, 0, jnp.sum(gain_sum, axis=0, keepdims=True),
            jnp.sum(offset_sum, axis=0, keepdims=True),
        )
        send_round(2 + layer, 1)

    def stream_back(layer, center, inverse, counted):
        wait_round(2 + layer, 1)
        sbuf[2 + layer, d, 0] = smsg[2 + layer, 0]
        total = lax.fori_loop(
            0, n, lambda j, carry: carry + sbuf[2 + layer, j, 0], jnp.zeros((8, 128), f32),
            unroll=short,
        )
        gain_total, offset_total = unpack(total)
        emsg[2 * layer, 2:3, :] = gain_total
        emsg[2 * layer + 1, 2:3, :] = offset_total
        factor = norm_in[2 * layer : 2 * layer + 1, :] * inverse
        gain_part, offset_part = gain_total / counted, offset_total / counted
        target = gx if layer == 0 else g

        def body(rows, carry):
            scaled = (xs[layer, rows, :] - center) * inverse
            usable = usable_at(rows)
            target[rows, :] = g[rows, :] + factor * (
                dn[rows, :] - usable * (offset_part + scaled * gain_part)
            )

        rows_loop(body)

    convert_own()
    wait_round(0, 2)
    for layer in range(2):
        if layer == 1:
            local_moments(1, total)
            send_round(1, 1)
            turn(0)
            until(0, (arrive_sibling, 1))
            wait_round(1, 1)
        center, spread, counted = join_moments(layer)
        emsg[2 * layer, 3:4, :] = center
        emsg[2 * layer + 1, 3:4, :] = spread
        inverse = lax.rsqrt(spread + epsilon)
        rowbuf[2 * layer : 2 * layer + 1, :] = center
        rowbuf[2 * layer + 1 : 2 * layer + 2, :] = inverse
        total = forward(layer, center, inverse)

    store_out = pltpu.make_async_copy(xs.at[2], out_ref, lsem.at[10])
    store_grad = pltpu.make_async_copy(gx, grad_ref, lsem.at[11])
    store_out.start()

    load_g.wait()
    center, inverse = rowbuf[2:3, :], rowbuf[3:4, :]
    gate_back(1)
    mixed_back(1)
    states_back(1)
    backward_scan(1)
    normed_back(1, center, inverse)
    turn(1)
    glu_back(1)
    steps_before("c1")
    c_back(1)
    steps_before("b1")
    b_back(1)
    steps_before("stream1")
    stream_back(1, center, inverse, counted)

    center, inverse = rowbuf[0:1, :], rowbuf[1:2, :]
    for name, work in (
        ("gate0", lambda: gate_back(0)),
        ("glu0", lambda: glu_back(0)),
        ("mixed0", lambda: mixed_back(0)),
        ("states0", lambda: states_back(0)),
        ("c0", lambda: c_back(0)),
        ("scan0", lambda: backward_scan(0)),
        ("b0", lambda: b_back(0)),
        ("normed0", lambda: normed_back(0, center, inverse)),
    ):
        steps_before(name)
        work()

    def vector_round(j):
        return remote(vmsg, vbuf.at[d], sts.at[4, j], stq.at[4, j], (lax.rem(d + j, n), s))

    for layer in range(2):
        decay_back(layer)

    def go(j, carry):
        vector_round(j).start()
        return carry

    def owner_copy(j):
        to = lax.rem(s + j, 4)
        return remote(emsg.at[to], ebuf.at[s], secs.at[j], secr.at[j], (d, to))

    lax.fori_loop(1, n, go, 0)
    def rest(part):
        def of(role):
            steps = plans[role]["rest"]
            cuts = (0, len(steps) // 4, len(steps) // 2, len(steps))
            return steps[cuts[part] : cuts[part + 1]]

        return of

    by_role(rest(0))
    stream_back(0, center, inverse, counted)
    store_grad.start()
    by_role(rest(1))

    def arrived(j, carry):
        vector_round(j).wait()
        return carry

    lax.fori_loop(1, n, arrived, 0)
    vbuf[d] = vmsg[...]
    total = lax.fori_loop(0, n, lambda j, carry: carry + vbuf[j], jnp.zeros((8, D), f32))
    for q in range(4):
        emsg[q, 0:2, :] = total[2 * q : 2 * q + 2, :]
    for j in range(1, 4):
        owner_copy(j).start()
    by_role(rest(2))

    for j in range(1, 4):
        owner_copy(j).wait()
    ebuf[s] = emsg[s]
    vector_total = jnp.zeros((2, D), f32)
    norm_total = jnp.zeros((1, D), f32)
    current = jnp.zeros((1, D), f32)
    for q in range(4):
        current = jnp.where(s == q, running_in[q : q + 1, :], current)
    for m in range(4):
        vector_total = vector_total + ebuf[m, 0:2, :]
        norm_total = norm_total + ebuf[m, 2:3, :]
        current = (1.0 - momentum) * current + momentum * ebuf[m, 3:4, :]
    vector_out[...] = vector_total
    norm_out[...] = norm_total
    running_out[...] = current

    for index in range(4):
        wait_round(index, 2 if index == 0 else 1, sent=True)
    for p in range(CHUNKS):
        own_copy(p).wait_send()
    for i in range(2 * CHUNKS):
        far_copy_of(i).wait_send()
        for kind in (2, 3, 4):
            hand_copy(kind, i).wait_send()
    for core in range(2):

        @pl.when(c == core)
        def _():
            for layer in range(2):
                for j in range(CHUNKS):
                    sibling_copy(core, layer, j).wait_send()

                    @pl.when(x != layer)
                    def _():
                        far_copy((layer, core, j)).wait_send()


    for j in range(CHUNKS):
        result_copy(j).wait()
    store_out.wait()
    store_grad.wait()


def finish(count, *refs):
    given, results, held, sems = refs[:count], refs[count : 2 * count], refs[2 * count : 3 * count], refs[-1]
    triples = []
    for triple in zip(given, held, results):
        rows = triple[0].shape[-2]
        if rows % 4 == 0 and rows >= 256:
            for part in range(4):
                cut = pl.ds(part * (rows // 4), rows // 4)
                triples.append([ref.at[0, cut] if len(ref.shape) == 3 else ref.at[cut] for ref in triple])
        else:
            triples.append(list(triple))
    first = [pltpu.make_async_copy(a, b, sems.at[0, i]) for i, (a, b, _) in enumerate(triples)]
    second = [pltpu.make_async_copy(b, e, sems.at[1, i]) for i, (_, b, e) in enumerate(triples)]
    for copy in first:
        copy.start()
    for copy, after in zip(first, second):
        copy.wait()
        after.start()
    for copy in second:
        copy.wait()


def solution(mesh):
    n = mesh.shape["dp"]
    k = n.bit_length() - 1
    assert mesh.shape["section"] == 4 and n == 1 << k and k >= 1

    def shards(block_input, cotangent, matrix, vectors, norm_params, running, resets, lengths):
        micro, rows, T, D = block_input.shape
        assert micro == 4 and rows == 1
        S = D // 2
        vmem = lambda shape, dtype=f32: pltpu.VMEM(shape, dtype)
        dma = lambda *shape: pltpu.SemaphoreType.DMA(shape)
        scratch = [
            vmem((3, T, D)), vmem((T, D)),
            vmem((4, 4, D, S)), vmem((4, D, 2 * D), bf16), vmem((4, D, 2 * D), bf16),
            vmem((2, T, D)), vmem((T, D), bf16), vmem((T, D), bf16),
            vmem((2, T, D)),
            vmem((2, T, D)), vmem((T, D), bf16), vmem((T, D), bf16),
            vmem((T, D)),
            vmem((2, T, D)),
            vmem((T, D), bf16), vmem((T, D), bf16),
            vmem((2, T, D)), vmem((2, T, D)),
            vmem((T, 2 * D), bf16), vmem((T, 2 * D), bf16),
            vmem((T, D)), vmem((T, D), bf16), vmem((T, D), bf16),
            vmem((T, D)),
            vmem((T, D), bf16), vmem((T, D), bf16),
            vmem((T, D)),
            vmem((4, 4, D, S)), vmem((2, 4, D, S)), vmem((2, 4, D, S)), vmem((4, D, S)),
            vmem((4, 2, D)),
            vmem((2, 4, 8, S)), vmem((2, 9, 8, S)),
            vmem((8, T, 128)), vmem((T, 128)),
            vmem((8, D)),
            vmem((4, 2, 8, 128)), vmem((4, n, 2, 8, 128)), vmem((8, 128)),
            vmem((8, D)), vmem((n, 8, D)), vmem((4, 4, D)), vmem((4, 4, D)),
            vmem((4, D, S)),
            *[vmem((2, D, T), bf16)] * 6,
            vmem((T, D)),
            vmem((2, 8, S)), vmem((2, 3, 8, S)),
            vmem((T, D)),
            dma(12), dma(5, 8), dma(5, 8), dma(2, 4), dma(2, 4),
            dma(2, 4, 3 * k + 1), dma(2, 4, 3 * k + 1), dma(4, 3 * k + 1), dma(4, 3 * k + 1),
            dma(5, n), dma(5, n), dma(4), dma(4), dma(4), dma(4),
        ]
        any_space = pl.BlockSpec(memory_space=pl.ANY)
        in_vmem = pl.BlockSpec(memory_space=pltpu.VMEM)
        in_smem = pl.BlockSpec(memory_space=pltpu.SMEM)
        shapes = (
            jax.ShapeDtypeStruct((T, D), f32),
            jax.ShapeDtypeStruct((T, D), f32),
            jax.ShapeDtypeStruct((1, D, 2 * D), f32),
            jax.ShapeDtypeStruct((2, D), f32),
            jax.ShapeDtypeStruct((1, D), f32),
            jax.ShapeDtypeStruct((1, D), f32),
        )
        results = pl.pallas_call(
            functools.partial(kernel, n, T, D),
            out_shape=shapes,
            in_specs=[any_space, any_space, any_space, in_vmem, in_vmem, in_vmem, in_smem, in_smem],
            out_specs=(any_space, any_space, any_space, in_vmem, in_vmem, in_vmem),
            scratch_shapes=scratch,
            compiler_params=pltpu.CompilerParams(
                collective_id=0, has_side_effects=True, vmem_limit_bytes=60 * 1024 * 1024
            ),
        )(block_input, cotangent, matrix, vectors, norm_params, running, resets, lengths.reshape(1, 4))
        out, grad, *rest = pl.pallas_call(
            functools.partial(finish, len(shapes)),
            out_shape=shapes,
            in_specs=[any_space] * len(shapes),
            out_specs=(any_space,) * len(shapes),
            scratch_shapes=[vmem(shape.shape) for shape in shapes] + [dma(2, 4 * len(shapes))],
        )(*results)
        return (out[None, None], grad[None, None], *rest)

    return jax.shard_map(
        shards,
        mesh=mesh,
        in_specs=(
            P(None, "dp", None, None),
            P(None, "dp", None, None),
            P("section", None, None),
            P("section", None),
            P(),
            P(),
            P(None, "dp", None),
            P(None, "dp"),
        ),
        out_specs=(
            P("section", "dp", None, None),
            P("section", "dp", None, None),
            P("section", None, None),
            P("section", None),
            P("section", None),
            P("section", None),
        ),
        check_vma=False,
    )
```
